128 devices in a mesh: lat: 8 (over x_hi, y), lon: 8 (over z, core), mp: 2 (over x_lo).
Axes of the slice: x: 4 (x_hi: 2, x_lo: 2; x = x_hi * 2 + x_lo), y: 4, z: 4, core: 2. Of those that a mesh axis runs over, the one named last changes fastest.
Arguments:
- fields: bfloat16 [256, 256, 512], P('lat', 'lon', 'mp'), may hold values from -6 to 6
- qkv_plain: bfloat16 [512, 3, 512], P(None, None, 'mp'), may hold values from -0.25 to 0.25
- out_plain: bfloat16 [512, 512], P('mp'), may hold values from -0.25 to 0.25
- qkv_shift: bfloat16 [512, 3, 512], P(None, None, 'mp'), may hold values from -0.25 to 0.25
- out_shift: bfloat16 [512, 512], P('mp'), may hold values from -0.25 to 0.25
- cotangent: bfloat16 [256, 256, 512], P('lat', 'lon', 'mp'), may hold values from -6 to 6
Outputs:
- result: bfloat16 [256, 256, 512], P('lat', 'lon', 'mp')
- grad_fields: bfloat16 [256, 256, 512], P('lat', 'lon', 'mp')
- grad_qkv_plain: float32 [512, 3, 512], P(None, None, 'mp')
- grad_out_plain: float32 [512, 512], P('mp')
- grad_qkv_shift: float32 [512, 3, 512], P(None, None, 'mp')
- grad_out_shift: float32 [512, 512], P('mp')
The draws below stay inside these ranges and needn't reach their ends.
All inputs are finite; a program needn't handle non-finite values.
Results may differ from the reference program's by a relative error of at most 0.034.
Values may be sent and summed in bfloat16 or wider, within the bound.
A program may use at most 128 MiB of HBM per device.

```python
import jax
import jax.numpy as jnp
from jax import lax

D = 512
HEAD_DIM = 32
WL = 8
WO = 16
NLAT = 256
NLON = 256
TOKENS = 65536
N_MP = 2


def block_scale(key, extent, cuts, smallest, high):
    level = 1.0
    for position, blocks in cuts:
        heights = jax.random.uniform(jax.random.fold_in(jax.random.fold_in(key, 6), position), (blocks,), jnp.float32, smallest / len(cuts), high / len(cuts))
        level = level * jnp.repeat(jnp.exp(heights), extent[position] // blocks).reshape((-1,) + (1,) * (len(extent) - 1 - position))
    return level


def scatter_about(rng, extent, deviation, reach, cuts=(), kind=jnp.bfloat16):
    drawn = jax.random.normal(rng, extent, jnp.float32) * deviation
    if len(cuts) > 0:
        drawn = block_scale(rng, extent, cuts, -0.22, 0.18) * drawn
    return jnp.clip(drawn, min=-reach, max=reach).astype(kind)


def setup_inputs(seed: int = 0) -> dict:
    seeds = jax.random.split(jax.random.key(seed), 7)
    fields = scatter_about(seeds[0], (NLAT, NLON, D), 1.0, 6.0, ((0, 8), (1, 8), (2, 2)))
    qkv_plain = scatter_about(seeds[1], (D, 3, D), D ** -0.5, 0.25, ((2, 2),))
    out_plain = scatter_about(seeds[2], (D, D), D ** -0.5, 0.25, ((0, 2),))
    qkv_shift = scatter_about(seeds[3], (D, 3, D), D ** -0.5, 0.25, ((2, 2),))
    out_shift = scatter_about(seeds[4], (D, D), D ** -0.5, 0.25, ((0, 2),))
    cotangent = scatter_about(seeds[5], (NLAT, NLON, D), 1.0, 6.0, ((0, 8), (1, 8), (2, 2)))
    return dict(fields=fields, qkv_plain=qkv_plain, out_plain=out_plain, qkv_shift=qkv_shift, out_shift=out_shift, cotangent=cotangent)


def to_windows(token_grid):
    grid_rows, grid_cols = (token_grid.shape[0], token_grid.shape[1])
    trailing = token_grid.shape[2:]
    blocked = token_grid.reshape((grid_rows // WL, WL, grid_cols // WO, WO) + trailing)
    perm_order = (0, 2, 1, 3) + tuple(range(4, 4 + len(trailing)))
    return blocked.transpose(perm_order).reshape((grid_rows // WL * (grid_cols // WO), WL * WO) + trailing)

def from_windows(windowed, grid_rows, grid_cols):
    trailing = windowed.shape[2:]
    blocked = windowed.reshape((grid_rows // WL, grid_cols // WO, WL, WO) + trailing)
    perm_order = (0, 2, 1, 3) + tuple(range(4, 4 + len(trailing)))
    return blocked.transpose(perm_order).reshape((grid_rows, grid_cols) + trailing)

def normalize(token_grid):
    average = lax.optimization_barrier(jnp.mean(token_grid, -1, keepdims=True))
    centred = token_grid - average
    inv_scale = lax.rsqrt(lax.optimization_barrier(jnp.mean(centred * centred, -1, keepdims=True)) + 1e-05)
    return (centred * inv_scale, inv_scale)

def norm_back(standard, inv_scale, gradient):
    return inv_scale * (gradient - lax.optimization_barrier(jnp.mean(gradient, -1, keepdims=True)) - standard * lax.optimization_barrier(jnp.mean(gradient * standard, -1, keepdims=True)))

def product(pattern, left_operand, right_operand):
    return jnp.einsum(pattern, left_operand.astype(jnp.float32), right_operand.astype(jnp.float32), precision=lax.Precision.HIGHEST)

def attention_core(projected, band_windows):
    windows, win_size = (projected.shape[0], projected.shape[1])
    head_count = projected.shape[3] // HEAD_DIM
    blocked = projected.reshape(windows, win_size, 3, head_count, HEAD_DIM)
    queries, key_part, values = (blocked[:, :, 0], blocked[:, :, 1], blocked[:, :, 2])
    scores = product('wqhe,wkhe->whqk', queries, key_part) * HEAD_DIM ** (-0.5)
    same_band = (band_windows[:, :, None] == band_windows[:, None, :])[:, None]
    raised = jnp.where(same_band, jnp.exp(scores), 0.0)
    softmax = (raised / lax.optimization_barrier(jnp.sum(raised, -1, keepdims=True))).astype(jnp.bfloat16)
    mixture = product('whqk,wkhe->wqhe', softmax, values).astype(jnp.bfloat16)
    return mixture.reshape(windows, win_size, head_count * HEAD_DIM)

def group_forward(normed, band_windows, qkv_weight, out_weight):
    projected = product('wtd,dce->wtce', normed, qkv_weight).astype(jnp.bfloat16)
    mixture, core_back = jax.vjp(lambda projected_in: attention_core(projected_in, band_windows), projected)
    partial_value = product('wte,ed->wtd', mixture, out_weight)
    return (partial_value, (mixture, core_back))

def group_backward(normed, stored, qkv_weight, out_weight, gradient):
    mixture, core_back = stored
    grad_out = product('wte,wtd->ed', mixture, gradient)
    grad_mixture = product('wtd,ed->wte', gradient, out_weight).astype(jnp.bfloat16)
    grad_projected = core_back(grad_mixture)[0]
    grad_qkv = product('wtd,wtce->dce', normed, grad_projected)
    grad_normed = product('wtce,dce->wtd', grad_projected, qkv_weight)
    return (grad_normed, grad_qkv, grad_out)

def rounded(quantity):
    return lax.optimization_barrier(quantity.astype(jnp.bfloat16)).astype(jnp.float32)

def block_forward(token_grid, band_grid, groups):
    grid_rows, grid_cols = (token_grid.shape[0], token_grid.shape[1])
    standard, inv_scale = normalize(token_grid)
    normed = to_windows(standard.astype(jnp.bfloat16))
    band_windows = to_windows(band_grid)
    partials, stored_list = ([], [])
    for qkv_weight, out_weight in groups:
        partial_value, stored = group_forward(normed, band_windows, qkv_weight, out_weight)
        partials.append(from_windows(partial_value, grid_rows, grid_cols))
        stored_list.append(stored)
    return (partials, (standard, inv_scale, normed, stored_list))

def block_backward(stored_block, groups, grad_grid):
    standard, inv_scale, normed, stored_list = stored_block
    grid_rows, grid_cols = (standard.shape[0], standard.shape[1])
    grad_windows = to_windows(grad_grid)
    summed = jnp.zeros(standard.shape, jnp.float32)
    qkv_list, out_list = ([], [])
    for stored, (qkv_weight, out_weight) in zip(stored_list, groups):
        grad_normed, grad_qkv, grad_out = group_backward(normed, stored, qkv_weight, out_weight, grad_windows)
        summed = summed + rounded(norm_back(standard, inv_scale, from_windows(grad_normed, grid_rows, grid_cols)))
        qkv_list.append(grad_qkv)
        out_list.append(grad_out)
    return (summed, jnp.concatenate(qkv_list, 2), jnp.concatenate(out_list, 0))

def make_groups(qkv_weight, out_weight):
    group_width = D // N_MP
    return [(qkv_weight[:, :, head_group * group_width:(head_group + 1) * group_width], out_weight[head_group * group_width:(head_group + 1) * group_width]) for head_group in range(N_MP)]

def reference(fields, qkv_plain, out_plain, qkv_shift, out_shift, cotangent):
    half_lat, half_lon = (WL // 2, WO // 2)
    plain_groups = make_groups(qkv_plain, out_plain)
    shift_groups = make_groups(qkv_shift, out_shift)
    plain_bands = jnp.ones((NLAT, NLON), jnp.int32)
    stream = fields.astype(jnp.float32)
    partials_plain, stored_plain = block_forward(stream, plain_bands, plain_groups)
    summed_plain = jnp.zeros(stream.shape, jnp.float32)
    for partial_grid in partials_plain:
        summed_plain = summed_plain + rounded(partial_grid)
    hidden = (stream + summed_plain).astype(jnp.bfloat16)
    hidden_wide = hidden.astype(jnp.float32)
    extended = jnp.concatenate([hidden_wide[:, NLON - half_lon:], hidden_wide, hidden_wide[:, :half_lon]], 1)
    extended = jnp.pad(extended, ((half_lat, half_lat), (0, 0), (0, 0)))
    row_ids = jnp.pad(jnp.ones((NLAT,), jnp.int32), (half_lat, half_lat))
    shift_bands = jnp.broadcast_to(row_ids[:, None], (NLAT + WL, NLON + WO))
    partials_shift, stored_shift = block_forward(extended, shift_bands, shift_groups)
    summed_shift = jnp.zeros(stream.shape, jnp.float32)
    for partial_grid in partials_shift:
        summed_shift = summed_shift + rounded(partial_grid[half_lat:half_lat + NLAT, half_lon:half_lon + NLON])
    result = (hidden_wide + summed_shift).astype(jnp.bfloat16)
    padded = jnp.pad(cotangent, ((half_lat, half_lat), (half_lon, half_lon), (0, 0)))
    back_shift, qkv_grad_shift, out_grad_shift = block_backward(stored_shift, shift_groups, padded)
    trimmed = back_shift[half_lat:half_lat + NLAT]
    centre = trimmed[:, half_lon:half_lon + NLON]
    centre = centre.at[:, :half_lon].add(trimmed[:, half_lon + NLON:])
    centre = centre.at[:, NLON - half_lon:].add(trimmed[:, :half_lon])
    grad_hidden = (cotangent.astype(jnp.float32) + centre).astype(jnp.bfloat16)
    back_plain, qkv_grad_plain, out_grad_plain = block_backward(stored_plain, plain_groups, grad_hidden)
    grad_fields = (grad_hidden.astype(jnp.float32) + back_plain).astype(jnp.bfloat16)
    factor = lax.rsqrt(jnp.float32(TOKENS))
    return (result, grad_fields, qkv_grad_plain * factor, out_grad_plain * factor, qkv_grad_shift * factor, out_grad_shift * factor)
```

```python
import functools

import jax
import jax.numpy as jnp
from jax import lax
from jax.experimental import pallas as pl
from jax.experimental.pallas import tpu as pltpu
from jax.sharding import PartitionSpec as P

BF = jnp.bfloat16
F32 = jnp.float32
MESH = pl.DeviceIdType.MESH
VMEM_LIMIT = 56 * 1024 * 1024
D = 512
HEAD_DIM = 32
SCALE = HEAD_DIM ** -0.5
LOG2E = 1.4426950408889634


def place():
    lat, lon, mp = lax.axis_index("lat"), lax.axis_index("lon"), lax.axis_index("mp")
    return lat, lon, mp


def row_step(lat, mp, step):
    at = lax.rem(lat * 2 + mp + step + 16, 16)
    return at // 2, lax.rem(at, 2)


def barrier(peers):
    sem = pltpu.get_barrier_semaphore()
    for peer in peers:
        pl.semaphore_signal(sem, inc=1, device_id=peer, device_id_type=MESH)
    pl.semaphore_wait(sem, len(peers))


class Sender:
    def __init__(self, send, recv):
        self.send, self.recv, self.used = send, recv, 0

    def __call__(self, src, dst, peer):
        copy = pltpu.make_async_remote_copy(
            src_ref=src,
            dst_ref=dst,
            send_sem=self.send.at[self.used],
            recv_sem=self.recv.at[self.used],
            device_id=peer,
            device_id_type=MESH,
        )
        self.used += 1
        copy.start()
        return copy


def comm_call(kernel, out_shape, sends, collective_id, scratch=(), locals_=1):
    vmem = pl.BlockSpec(memory_space=pltpu.VMEM)

    def call(*args):
        return pl.pallas_call(
            kernel,
            out_shape=out_shape,
            in_specs=[vmem] * len(args),
            out_specs=[vmem] * len(out_shape),
            scratch_shapes=[
                *scratch,
                pltpu.SemaphoreType.DMA((sends,)),
                pltpu.SemaphoreType.DMA((sends,)),
                pltpu.SemaphoreType.DMA((locals_,)),
            ],
            compiler_params=pltpu.CompilerParams(
                collective_id=collective_id,
                has_side_effects=True,
                vmem_limit_bytes=VMEM_LIMIT,
            ),
        )(*args)

    return call


def enter_kernel(
    fc, cc, wqp, wop, wqs, wos, x, c, fqp, fop, fqs, fos, send, recv, local
):
    lat, lon, mp = place()
    near = (lat, lon, 1 - mp)
    far = (lax.rem(lat + 4, 8), lon, 1 - mp)
    core = lax.rem(lon, 2)
    sibling = (lat, lon + 1 - 2 * core, mp)
    barrier([near, far, sibling])
    go = Sender(send, recv)
    lanes = pl.ds(pl.multiple_of(mp * 256, 256), 256)
    other_rows = pl.ds((1 - mp) * 4, 4)
    own_rows = pl.ds(mp * 4, 4)
    first = [go(fc.at[other_rows], x.at[:, :, :, lanes], near)]
    kept = []
    for n, (src, dst) in enumerate(
        (
            (fc.at[own_rows], x.at[:, :, :, lanes]),
            (cc.at[own_rows], c.at[:, :, :, lanes]),
            (wqp, fqp.at[:, :, lanes]),
            (wqs, fqs.at[:, :, lanes]),
            (wop, fop.at[pl.ds(pl.multiple_of(mp * 256, 256), 256)]),
            (wos, fos.at[pl.ds(pl.multiple_of(mp * 256, 256), 256)]),
        )
    ):
        copy = pltpu.make_async_copy(src, dst, local.at[n])
        copy.start()
        kept.append(copy)
    peers = (near, far)
    mine, theirs = [], []
    for src, dst in ((wqp, fqp), (wqs, fqs)):
        for k in range(2):
            rows = pl.ds(pl.multiple_of((k * 2 + core) * 128, 128), 128)
            mine.append((go(src.at[:, rows], dst.at[:, rows, lanes], peers[k]), dst, rows, None))
    for src, dst in ((wop, fop), (wos, fos)):
        for k in range(2):
            rows = pl.ds(pl.multiple_of((k * 2 + core) * 64, 64), 64)
            there = pl.ds(pl.multiple_of(mp * 256 + (k * 2 + core) * 64, 64), 64)
            here = pl.ds(pl.multiple_of((1 - mp) * 256 + (k * 2 + core) * 64, 64), 64)
            mine.append((go(src.at[rows], dst.at[there], peers[k]), dst, None, here))
    first.append(go(cc.at[other_rows], c.at[:, :, :, lanes], near))
    arrived = pl.ds(pl.multiple_of((1 - mp) * 256, 256), 256)
    for copy, dst, rows, here in mine:
        copy.wait_recv()
        spot = dst.at[here] if rows is None else dst.at[:, rows, arrived]
        theirs.append(go(spot, spot, sibling))
    for copy, _, _, _ in mine:
        copy.wait_send()
    for copy in first + theirs:
        copy.wait()
    for copy in kept:
        copy.wait()


def around(lat, lon, mp, step):
    row_lat, row_mp = row_step(lat, mp, step)
    col = lax.rem(lon + step + 8, 8)
    return (row_lat, row_lat * 0 + lon, row_mp), (lat, col, mp), (row_lat, col, row_mp)


def widen_kernel(h, c, hx, cx, send, recv, local):
    lat, lon, mp = place()
    row_prev, col_prev, corner_prev = around(lat, lon, mp, -1)
    row_next, col_next, corner_next = around(lat, lon, mp, 1)
    barrier([row_prev, col_prev, corner_prev, row_next, col_next, corner_next])
    go = Sender(send, recv)
    copies = []
    for src, dst in ((h, hx), (c, cx)):
        copies.append(go(src.at[0], dst.at[4, pl.ds(0, 4)], row_prev))
        copies.append(go(src.at[:, 0], dst.at[pl.ds(0, 4), 4], col_prev))
        copies.append(go(src.at[0, 0], dst.at[4, 4], corner_prev))
    for n, (src, dst) in enumerate(((h, hx), (c, cx))):
        copy = pltpu.make_async_copy(src, dst.at[pl.ds(0, 4), pl.ds(0, 4)], local.at[n])
        copy.start()
        copies.append(copy)
    for copy in copies:
        copy.wait()


def narrow_kernel(a, b, ao, bo, send, recv, local):
    lat, lon, mp = place()
    row_prev, col_prev, corner_prev = around(lat, lon, mp, -1)
    row_next, col_next, corner_next = around(lat, lon, mp, 1)
    barrier([row_prev, col_prev, corner_prev, row_next, col_next, corner_next])
    go = Sender(send, recv)
    copies = []
    low, high = pl.ds(0, 3), pl.ds(1, 3)
    for src, dst in ((a, ao), (b, bo)):
        copies.append(go(src.at[3, low], dst.at[0, high], row_next))
        copies.append(go(src.at[low, 3], dst.at[high, 0], col_next))
        copies.append(go(src.at[3, 3], dst.at[0, 0], corner_next))
    for n, (src, dst) in enumerate(((a, ao), (b, bo))):
        copy = pltpu.make_async_copy(src.at[low, low], dst.at[high, high], local.at[n])
        copy.start()
        copies.append(copy)
    for copy in copies:
        copy.wait()


def leave_kernel(
    r, gf, g, ro, gfo, out, r0, a0, r1, a1, r2, a2, r3, f, send, recv, local
):
    lat, lon, mp = place()
    core, z = lax.rem(lon, 2), lon // 2
    y, x_hi = lax.rem(lat, 4), lat // 4
    near = (lat, lon, 1 - mp)
    far = (lax.rem(lat + 4, 8), lon, 1 - mp)
    opposite = (lax.rem(lat + 4, 8), lon, mp)
    sibling = (lat, lon + 1 - 2 * core, mp)

    def along_y(step):
        return (x_hi * 4 + lax.rem(y + step, 4), lon, mp)

    def along_z(step):
        return (lat, lax.rem(z + step, 4) * 2 + core, mp)

    barrier(
        [near, far, opposite, sibling]
        + [along_y(s) for s in (1, 2, 3)]
        + [along_z(s) for s in (1, 2, 3)]
    )
    go = Sender(send, recv)
    lanes = pl.ds(pl.multiple_of(mp * 256, 256), 256)
    away = pl.ds(pl.multiple_of((1 - mp) * 256, 256), 256)
    own_rows = pl.ds(mp * 4, 4)
    s0 = go(g.at[:, :, 1 - core], r0, sibling)
    late = [
        go(gf.at[:, :, :, away], gfo.at[own_rows], near),
        go(r.at[:, :, :, away], ro.at[own_rows], near),
    ]
    for n, (src, dst) in enumerate(((r, ro), (gf, gfo))):
        copy = pltpu.make_async_copy(src.at[:, :, :, lanes], dst.at[own_rows], local.at[n])
        copy.start()
        late.append(copy)
    s0.wait()

    ways = ((y, along_y, z, along_z), (z, along_z, y, along_y))

    def fold0(n, carry):
        block, part, a = n // 8, lax.rem(n // 4, 2), lax.rem(n, 4)
        mine = g[block, :, core, part, a].astype(F32)
        a0[block, :, part, a] = (mine + r0[block, :, part, a].astype(F32)).astype(BF)
        return carry

    lax.fori_loop(0, 16, fold0, 0)
    s1 = []
    for part, (ia, along_a, ib, along_b) in enumerate(ways):
        for step in (1, 2, 3):
            to = lax.rem(ia + step, 4)
            s1.append(go(a0.at[:, :, part, to], r1.at[part, step - 1], along_a(step)))
    for copy in s1:
        copy.wait()
    for part, (ia, along_a, ib, along_b) in enumerate(ways):

        def fold1(b, carry):
            total = a0[:, :, part, ia, b].astype(F32)
            for k in range(3):
                total = total + r1[part, k, :, :, b].astype(F32)
            a1[:, :, part, b] = total.astype(BF)
            return carry

        lax.fori_loop(0, 4, fold1, 0)
    s2 = []
    for part, (ia, along_a, ib, along_b) in enumerate(ways):
        for step in (1, 2, 3):
            to = lax.rem(ib + step, 4)
            s2.append(go(a1.at[:, :, part, to], r2.at[part, step - 1], along_b(step)))
    for copy in s2:
        copy.wait()
    for part, (ia, along_a, ib, along_b) in enumerate(ways):
        total = a1[:, :, part, ib].astype(F32)
        for k in range(3):
            total = total + r2[part, k].astype(F32)
        a2[:, :, part] = total.astype(BF)
    s3 = [
        go(a2.at[:, 1 - mp, :, x_hi], r3.at[0], near),
        go(a2.at[:, 1 - mp, :, 1 - x_hi], r3.at[1], far),
        go(a2.at[:, mp, :, 1 - x_hi], r3.at[2], opposite),
    ]
    for copy in s3:
        copy.wait()
    total = a2[:, mp, :, x_hi].astype(F32)
    for k in range(3):
        total = total + r3[k].astype(F32)
    total = total.astype(BF)
    for part, (ia, along_a, ib, along_b) in enumerate(ways):
        f[core, part, ia, ib, x_hi] = total[:, part]
    s4 = []
    for part, (ia, along_a, ib, along_b) in enumerate(ways):
        spot = f.at[core, part, ia, ib, x_hi]
        s4.append(go(spot, spot, opposite))
    for copy in s4:
        copy.wait()
    s5 = []
    for part, (ia, along_a, ib, along_b) in enumerate(ways):
        spot = f.at[core, part, ia, ib]
        for step in (1, 2, 3):
            s5.append(go(spot, spot, along_b(step)))
    for copy in s5:
        copy.wait()
    s6 = []
    for part, (ia, along_a, ib, along_b) in enumerate(ways):
        spot = f.at[core, part, ia]
        for step in (1, 2, 3):
            s6.append(go(spot, spot, along_a(step)))
    for copy in s6:
        copy.wait()
    spot = f.at[core]
    s7 = go(spot, spot, sibling)
    s7.wait()

    factor = 1.0 / 256.0

    def spread(n, carry):
        half, part, a = n // 8, lax.rem(n // 4, 2), lax.rem(n, 4)
        value = f[half, part, a].astype(F32) * factor
        for block in range(2):
            out[block, half, part, a] = value[:, :, block]
        return carry

    lax.fori_loop(0, 16, spread, 0)
    for copy in late:
        copy.wait()


NN = (((1,), (0,)), ((), ()))
NT = (((1,), (1,)), ((), ()))
TN = (((0,), (0,)), ((), ()))


def dot(left, right, dims=NN):
    return lax.dot_general(left, right, dims, preferred_element_type=F32)


def head_masks():
    lane = lax.broadcasted_iota(jnp.int32, (128, 128), 1) // HEAD_DIM
    return [lane == h for h in range(4)]


def spread_heads(block, masks):
    zero = jnp.zeros_like(block)
    return jnp.concatenate([jnp.where(m, block, zero) for m in masks], 0)


def merge_heads(tall, masks):
    total = jnp.where(masks[0], tall[0:128], 0.0)
    for h in range(1, 4):
        total = jnp.where(masks[h], tall[h * 128 : (h + 1) * 128], total)
    return total


def standardize(x):
    centred = x - jnp.mean(x, -1, keepdims=True)
    inv = lax.rsqrt(jnp.mean(centred * centred, -1, keepdims=True) + 1e-05)
    return centred * inv, inv


def window(ref, w, offset):
    i, j = w // 2, lax.rem(w, 2)
    got = ref[pl.ds(2 * i + offset, 2), pl.ds(2 * j + offset, 2)]
    return got.reshape(128, D)


def put_window(ref, w, value):
    i, j = w // 2, lax.rem(w, 2)
    ref[pl.ds(2 * i, 2), pl.ds(2 * j, 2)] = value.reshape(2, 2, 32, D)


def forward(x, offset, wq, wo, n, pr, es, rd, mix, out, cut):
    def norm(w, carry):
        n[w] = standardize(window(x, w, offset).astype(F32))[0].astype(BF)
        return carry

    lax.fori_loop(0, 4, norm, 0)
    for c in range(3):
        for j in range(2):
            got = dot(n[...].reshape(512, 512), wq[c, :, j * 256 : (j + 1) * 256])
            pr[:, :, c * 512 + j * 256 : c * 512 + (j + 1) * 256] = got.astype(BF).reshape(4, 128, 256)

    masks = head_masks()
    ones = spread_heads(jnp.ones((128, 128), BF), masks)
    if cut is not None:
        q_half = lax.broadcasted_iota(jnp.int32, (128, 512), 0) // 64
        k_half = lax.rem(lax.broadcasted_iota(jnp.int32, (128, 512), 1) // 64, 2)
        same = q_half == k_half

    def attend(w, carry):
        for s in range(4):
            q = pr[w, :, s * 128 : (s + 1) * 128]
            k = spread_heads(pr[w, :, 512 + s * 128 : 512 + (s + 1) * 128], masks)
            v = spread_heads(pr[w, :, 1024 + s * 128 : 1024 + (s + 1) * 128], masks)
            e = jnp.exp2(dot(q, k, NT) * (SCALE * LOG2E))
            if cut is not None:
                e = jnp.where(same | jnp.logical_not(cut & (w >= 2)), e, 0.0)
            e = e.astype(BF)
            es[w, s] = e
            both = dot(e, jnp.concatenate([v, ones], 1))
            inv = 1.0 / both[:, 128:]
            rd[w, :, s * 128 : (s + 1) * 128] = inv
            mix[w, :, s * 128 : (s + 1) * 128] = (both[:, :128] * inv).astype(BF)
        return carry

    lax.fori_loop(0, 4, attend, 0)

    def project(w, carry):
        value = window(x, w, offset).astype(F32) + dot(mix[w], wo[...])
        put_window(out, w, value.astype(BF))
        return carry

    lax.fori_loop(0, 4, project, 0)


def backward(x, offset, ct, ct_offset, wq, wo, n, pr, es, rd, mix, cw, do, dpr, out, g):
    def gather(w, carry):
        cw[w] = window(ct, w, ct_offset)
        return carry

    lax.fori_loop(0, 4, gather, 0)
    for j in range(2):
        cols = slice(j * 256, (j + 1) * 256)
        got = dot(cw[...].reshape(512, 512), wo[cols, :], NT)
        do[:, :, cols] = got.reshape(4, 128, 256)
        got = dot(mix[:, :, cols].reshape(512, 256), cw[...].reshape(512, 512), TN).astype(BF)
        g[j, 1536:1792] = got[:, 0:256]
        g[j, 1792:2048] = got[:, 256:512]

    masks = head_masks()
    ones = spread_heads(jnp.ones((128, 128), BF), masks)

    def attend(w, carry):
        for s in range(4):
            lanes = slice(s * 128, (s + 1) * 128)
            q = pr[w, :, lanes]
            k = spread_heads(pr[w, :, 512 + s * 128 : 512 + (s + 1) * 128], masks)
            v = spread_heads(pr[w, :, 1024 + s * 128 : 1024 + (s + 1) * 128], masks)
            e = es[w, s]
            g1 = do[w, :, lanes] * rd[w, :, lanes]
            g2 = g1 * mix[w, :, lanes].astype(F32)
            g1 = g1.astype(BF)
            t = dot(jnp.concatenate([g1, (-g2).astype(BF)], 1), jnp.concatenate([v, ones], 1), NT)
            ds = (e.astype(F32) * t).astype(BF)
            dq = dot(ds, k) * SCALE
            dk = merge_heads(dot(ds, q, TN), masks) * SCALE
            dv = merge_heads(dot(e, g1, TN), masks)
            dpr[w, :, lanes] = dq.astype(BF)
            dpr[w, :, 512 + s * 128 : 512 + (s + 1) * 128] = dk.astype(BF)
            dpr[w, :, 1024 + s * 128 : 1024 + (s + 1) * 128] = dv.astype(BF)
        return carry

    lax.fori_loop(0, 4, attend, 0)
    for c in range(3):
        for j in range(2):
            cols = slice(c * 512 + j * 256, c * 512 + (j + 1) * 256)
            got = dot(n[...].reshape(512, 512), dpr[:, :, cols].reshape(512, 256), TN)
            g[j, c * 512 : (c + 1) * 512] = got.astype(BF)

    def finish(w, carry):
        grad = dot(dpr[w, :, 0:512], wq[0], NT)
        grad = grad + dot(dpr[w, :, 512:1024], wq[1], NT)
        grad = grad + dot(dpr[w, :, 1024:1536], wq[2], NT)
        standard, inv = standardize(window(x, w, offset).astype(F32))
        back = inv * (
            grad
            - jnp.mean(grad, -1, keepdims=True)
            - standard * jnp.mean(grad * standard, -1, keepdims=True)
        )
        put_window(out, w, (cw[w].astype(F32) + back).astype(BF))
        return carry

    lax.fori_loop(0, 4, finish, 0)


def plain_forward_kernel(x, wq, wo, out, n, pr, es, rd, mix):
    forward(x, 0, wq, wo, n, pr, es, rd, mix, out, None)


def shift_kernel(x, ct, wq, wo, out, back, g, n, pr, es, rd, mix, cw, do, dpr):
    lat, lon, mp = place()
    cut = (lat * 2 + mp) == 15
    forward(x, 1, wq, wo, n, pr, es, rd, mix, out, cut)
    backward(x, 1, ct, 1, wq, wo, n, pr, es, rd, mix, cw, do, dpr, back, g)


def plain_backward_kernel(x, ct, wq, wo, n, pr, es, rd, mix, back, g, cw, do, dpr):
    backward(x, 0, ct, 0, wq, wo, n, pr, es, rd, mix, cw, do, dpr, back, g)


def shape(*dims, dtype=BF):
    return jax.ShapeDtypeStruct(dims, dtype)


SAVED = ((4, 128, 512), BF), ((4, 128, 1536), BF), ((4, 4, 128, 512), BF), ((4, 128, 512), F32), ((4, 128, 512), BF)
WORK = ((4, 128, 512), BF), ((4, 128, 512), F32), ((4, 128, 1536), BF)


def compute_call(kernel, out_shape, scratch=()):
    vmem = pl.BlockSpec(memory_space=pltpu.VMEM)

    def call(*args):
        return pl.pallas_call(
            kernel,
            out_shape=out_shape,
            in_specs=[vmem] * len(args),
            out_specs=[vmem] * len(out_shape),
            scratch_shapes=[pltpu.VMEM(s, t) for s, t in scratch],
            compiler_params=pltpu.CompilerParams(vmem_limit_bytes=VMEM_LIMIT),
        )(*args)

    return call


def cells(tokens):
    return tokens.reshape(8, 4, 4, 8, 256).transpose(0, 2, 1, 3, 4).reshape(8, 4, 32, 256)


def uncells(tokens):
    return tokens.reshape(8, 4, 4, 8, 256).transpose(0, 2, 1, 3, 4).reshape(32, 32, 256)


def on_device(fields, qkv_plain, out_plain, qkv_shift, out_shift, cotangent):
    grid = shape(4, 4, 32, 512)
    wide = shape(5, 5, 32, 512)
    wq, wo = shape(3, 512, 512), shape(512, 512)
    x, c, wqp, wop, wqs, wos = comm_call(
        enter_kernel, [grid, grid, wq, wo, wq, wo], 18, 0, locals_=6
    )(
        cells(fields),
        cells(cotangent),
        qkv_plain.transpose(1, 0, 2),
        out_plain,
        qkv_shift.transpose(1, 0, 2),
        out_shift,
    )
    hidden, *saved = compute_call(
        plain_forward_kernel, [grid] + [shape(*s, dtype=t) for s, t in SAVED]
    )(x, wqp, wop)
    hx, cx = comm_call(widen_kernel, [wide, wide], 6, 1, locals_=2)(hidden, c)
    grads = shape(2, 2048, 256)
    shifted_result, shifted_grad, g_shift = compute_call(
        shift_kernel, [grid, grid, grads], SAVED + WORK
    )(hx, cx, wqs, wos)
    result, grad_hidden = comm_call(narrow_kernel, [grid, grid], 6, 2, locals_=2)(
        shifted_result, shifted_grad
    )
    grad_fields, g_plain = compute_call(plain_backward_kernel, [grid, grads], WORK)(
        x, grad_hidden, wqp, wop, *saved
    )
    g = jnp.stack([g_plain, g_shift]).reshape(2, 2, 2, 2, 4, 4, 2, 16, 256)
    held = shape(8, 4, 32, 256)
    result, grad_fields, sums = comm_call(
        leave_kernel,
        [held, held, shape(2, 2, 2, 4, 4, 2, 16, 256, dtype=F32)],
        34,
        3,
        scratch=(
            pltpu.VMEM((2, 2, 2, 4, 4, 2, 16, 256), BF),
            pltpu.VMEM((2, 2, 2, 4, 4, 2, 16, 256), BF),
            pltpu.VMEM((2, 3, 2, 2, 4, 2, 16, 256), BF),
            pltpu.VMEM((2, 2, 2, 4, 2, 16, 256), BF),
            pltpu.VMEM((2, 3, 2, 2, 2, 16, 256), BF),
            pltpu.VMEM((2, 2, 2, 2, 16, 256), BF),
            pltpu.VMEM((3, 2, 2, 16, 256), BF),
            pltpu.VMEM((2, 2, 4, 4, 2, 2, 16, 256), BF),
        ),
        locals_=2,
    )(result, grad_fields, g)
    sums = sums.reshape(2, 2048, 256)
    outs = []
    for block in range(2):
        outs.append(sums[block, :1536].reshape(3, 512, 256).transpose(1, 0, 2))
        outs.append(jnp.concatenate([sums[block, 1536:1792], sums[block, 1792:]], 1))
    return (uncells(result), uncells(grad_fields), *outs)


def solution(mesh):
    in_specs = (
        P("lat", "lon", "mp"),
        P(None, None, "mp"),
        P("mp", None),
        P(None, None, "mp"),
        P("mp", None),
        P("lat", "lon", "mp"),
    )
    out_specs = (
        P("lat", "lon", "mp"),
        P("lat", "lon", "mp"),
        P(None, None, "mp"),
        P("mp", None),
        P(None, None, "mp"),
        P("mp", None),
    )
    return jax.shard_map(
        on_device, mesh=mesh, in_specs=in_specs, out_specs=out_specs, check_vma=False
    )
```

```python
import functools

import jax
import jax.numpy as jnp
from jax import lax
from jax.experimental import pallas as pl
from jax.experimental.pallas import tpu as pltpu
from jax.sharding import PartitionSpec as P

BF = jnp.bfloat16
F32 = jnp.float32
MESH = pl.DeviceIdType.MESH
VMEM_LIMIT = 56 * 1024 * 1024
D = 512
HEAD_DIM = 32
SCALE = HEAD_DIM ** -0.5
LOG2E = 1.4426950408889634


def place():
    lat, lon, mp = lax.axis_index("lat"), lax.axis_index("lon"), lax.axis_index("mp")
    return lat, lon, mp


def row_step(lat, mp, step):
    at = lax.rem(lat * 2 + mp + step + 16, 16)
    return at // 2, lax.rem(at, 2)


def barrier(peers):
    sem = pltpu.get_barrier_semaphore()
    for peer in peers:
        pl.semaphore_signal(sem, inc=1, device_id=peer, device_id_type=MESH)
    pl.semaphore_wait(sem, len(peers))


class Sender:
    def __init__(self, send, recv):
        self.send, self.recv, self.used = send, recv, 0

    def __call__(self, src, dst, peer):
        copy = pltpu.make_async_remote_copy(
            src_ref=src,
            dst_ref=dst,
            send_sem=self.send.at[self.used],
            recv_sem=self.recv.at[self.used],
            device_id=peer,
            device_id_type=MESH,
        )
        self.used += 1
        copy.start()
        return copy


NN = (((1,), (0,)), ((), ()))
NT = (((1,), (1,)), ((), ()))
TN = (((0,), (0,)), ((), ()))


def dot(left, right, dims=NN):
    return lax.dot_general(left, right, dims, preferred_element_type=F32)


def head_masks():
    lane = lax.broadcasted_iota(jnp.int32, (128, 128), 1) // HEAD_DIM
    return [lane == h for h in range(4)]


def spread_heads(block, masks):
    zero = jnp.zeros_like(block)
    return jnp.concatenate([jnp.where(m, block, zero) for m in masks], 0)


def merge_heads(tall, masks):
    total = jnp.where(masks[0], tall[0:128], 0.0)
    for h in range(1, 4):
        total = jnp.where(masks[h], tall[h * 128 : (h + 1) * 128], total)
    return total


def standardize(x):
    centred = x - jnp.mean(x, -1, keepdims=True)
    inv = lax.rsqrt(jnp.mean(centred * centred, -1, keepdims=True) + 1e-05)
    return centred * inv, inv


def window(ref, w, offset):
    i, j = w // 2, lax.rem(w, 2)
    got = ref[pl.ds(2 * i + offset, 2), pl.ds(2 * j + offset, 2)]
    return got.reshape(128, D)


def put_window(ref, w, value):
    i, j = w // 2, lax.rem(w, 2)
    ref[pl.ds(2 * i, 2), pl.ds(2 * j, 2)] = value.reshape(2, 2, 32, D)


def forward_norm(x, offset, n, low, high):
    def norm(w, carry):
        n[w] = standardize(window(x, w, offset).astype(F32))[0].astype(BF)
        return carry

    lax.fori_loop(low, high, norm, 0)


def forward_project(n, wq, pr, low, high):
    count = high - low
    for c in range(3):
        for j in range(2):
            cols = slice(c * 512 + j * 256, c * 512 + (j + 1) * 256)
            got = dot(n[low:high].reshape(count * 128, 512), wq[c, :, j * 256 : (j + 1) * 256])
            pr[low:high, :, cols] = got.astype(BF).reshape(count, 128, 256)


def forward_attend(pr, es, rd, mix, cut, low, high):
    masks = head_masks()
    ones = spread_heads(jnp.ones((128, 128), BF), masks)
    if cut is not None:
        q_half = lax.broadcasted_iota(jnp.int32, (128, 512), 0) // 64
        k_half = lax.rem(lax.broadcasted_iota(jnp.int32, (128, 512), 1) // 64, 2)
        same = q_half == k_half

    def attend(w, carry):
        for s in range(4):
            q = pr[w, :, s * 128 : (s + 1) * 128]
            k = spread_heads(pr[w, :, 512 + s * 128 : 512 + (s + 1) * 128], masks)
            v = spread_heads(pr[w, :, 1024 + s * 128 : 1024 + (s + 1) * 128], masks)
            e = jnp.exp2(dot(q, k, NT) * (SCALE * LOG2E))
            if cut is not None:
                e = jnp.where(same | jnp.logical_not(cut & (w >= 2)), e, 0.0)
            e = e.astype(BF)
            es[w, s] = e
            both = dot(e, jnp.concatenate([v, ones], 1))
            inv = 1.0 / both[:, 128:]
            rd[w, :, s * 128 : (s + 1) * 128] = inv
            mix[w, :, s * 128 : (s + 1) * 128] = (both[:, :128] * inv).astype(BF)
        return carry

    lax.fori_loop(low, high, attend, 0)


def forward_out(x, offset, wo, mix, out, low, high):
    def project(w, carry):
        value = window(x, w, offset).astype(F32) + dot(mix[w], wo[...])
        put_window(out, w, value.astype(BF))
        return carry

    lax.fori_loop(low, high, project, 0)


def backward_out(ct, ct_offset, wo, mix, cw, do, g):
    def gather(w, carry):
        cw[w] = window(ct, w, ct_offset)
        return carry

    lax.fori_loop(0, 4, gather, 0)
    for j in range(2):
        cols = slice(j * 256, (j + 1) * 256)
        got = dot(cw[...].reshape(512, 512), wo[cols, :], NT)
        do[:, :, cols] = got.reshape(4, 128, 256)
    for j in range(2):
        cols = slice(j * 256, (j + 1) * 256)
        got = dot(mix[:, :, cols].reshape(512, 256), cw[...].reshape(512, 512), TN).astype(BF)
        g[j, 1, 1, 0:2] = got[:, 0:256].reshape(2, 4, 2, 16, 256)
        g[j, 1, 1, 2:4] = got[:, 256:512].reshape(2, 4, 2, 16, 256)


def backward_attend(pr, es, rd, mix, do, dpr, low, high):
    masks = head_masks()
    ones = spread_heads(jnp.ones((128, 128), BF), masks)

    def attend(w, carry):
        for s in range(4):
            lanes = slice(s * 128, (s + 1) * 128)
            q = pr[w, :, lanes]
            k = spread_heads(pr[w, :, 512 + s * 128 : 512 + (s + 1) * 128], masks)
            v = spread_heads(pr[w, :, 1024 + s * 128 : 1024 + (s + 1) * 128], masks)
            e = es[w, s]
            g1 = do[w, :, lanes] * rd[w, :, lanes]
            g2 = g1 * mix[w, :, lanes].astype(F32)
            g1 = g1.astype(BF)
            t = dot(jnp.concatenate([g1, (-g2).astype(BF)], 1), jnp.concatenate([v, ones], 1), NT)
            ds = (e.astype(F32) * t).astype(BF)
            dq = dot(ds, k) * SCALE
            dk = merge_heads(dot(ds, q, TN), masks) * SCALE
            dv = merge_heads(dot(e, g1, TN), masks)
            dpr[w, :, lanes] = dq.astype(BF)
            dpr[w, :, 512 + s * 128 : 512 + (s + 1) * 128] = dk.astype(BF)
            dpr[w, :, 1024 + s * 128 : 1024 + (s + 1) * 128] = dv.astype(BF)
        return carry

    lax.fori_loop(low, high, attend, 0)


def backward_weights(n, dpr, g):
    for c in range(3):
        for j in range(2):
            cols = slice(c * 512 + j * 256, c * 512 + (j + 1) * 256)
            got = dot(n[...].reshape(512, 512), dpr[:, :, cols].reshape(512, 256), TN)
            g[j, c // 2, c % 2] = got.astype(BF).reshape(4, 4, 2, 16, 256)


def backward_tokens(x, offset, wq, cw, dpr, out):
    def finish(w, carry):
        grad = dot(dpr[w, :, 0:512], wq[0], NT)
        grad = grad + dot(dpr[w, :, 512:1024], wq[1], NT)
        grad = grad + dot(dpr[w, :, 1024:1536], wq[2], NT)
        standard, inv = standardize(window(x, w, offset).astype(F32))
        back = inv * (
            grad
            - jnp.mean(grad, -1, keepdims=True)
            - standard * jnp.mean(grad * standard, -1, keepdims=True)
        )
        put_window(out, w, (cw[w].astype(F32) + back).astype(BF))
        return carry

    lax.fori_loop(0, 4, finish, 0)


class Sum:
    def __init__(self, go, g, f, r0, a0, r1, a1, r2, a2, r3):
        self.go, self.g, self.f = go, g, f
        self.r0, self.a0, self.r1, self.a1, self.r2, self.a2, self.r3 = r0, a0, r1, a1, r2, a2, r3
        lat, lon, mp = place()
        self.mp, self.core, z = mp, lax.rem(lon, 2), lon // 2
        y, self.x_hi = lax.rem(lat, 4), lat // 4
        self.near = (lat, lon, 1 - mp)
        self.far = (lax.rem(lat + 4, 8), lon, 1 - mp)
        self.opposite = (lax.rem(lat + 4, 8), lon, mp)
        self.sibling = (lat, lon + 1 - 2 * self.core, mp)

        def along_y(step):
            return (lat // 4 * 4 + lax.rem(y + step, 4), lon, mp)

        def along_z(step):
            return (lat, lax.rem(z + step, 4) * 2 + lax.rem(lon, 2), mp)

        self.ways = ((y, along_y, z, along_z), (z, along_z, y, along_y))
        self.peers = [self.near, self.far, self.opposite, self.sibling]
        self.peers += [along_y(s) for s in (1, 2, 3)] + [along_z(s) for s in (1, 2, 3)]
        self.flying = []

    def wait(self):
        for copy in self.flying:
            copy.wait()
        self.flying = []

    def step0(self):
        self.flying = [self.go(self.g.at[:, 1 - self.core], self.r0, self.sibling)]

    def step1(self):
        self.wait()
        g, r0, a0, core = self.g, self.r0, self.a0, self.core

        def fold(n, carry):
            part, a = n // 4, lax.rem(n, 4)
            mine = g[:, core, part, a].astype(F32)
            a0[:, part, a] = (mine + r0[:, part, a].astype(F32)).astype(BF)
            return carry

        lax.fori_loop(0, 8, fold, 0)
        for step in (1, 2, 3):
            for part, (ia, along_a, ib, along_b) in enumerate(self.ways):
                to = lax.rem(ia + step, 4)
                self.flying.append(
                    self.go(a0.at[:, part, to], self.r1.at[part, step - 1], along_a(step))
                )

    def step2(self):
        self.wait()
        a0, r1, a1 = self.a0, self.r1, self.a1
        for part, (ia, along_a, ib, along_b) in enumerate(self.ways):

            def fold(b, carry):
                total = a0[:, part, ia, b].astype(F32)
                for k in range(3):
                    total = total + r1[part, k, :, b].astype(F32)
                a1[:, part, b] = total.astype(BF)
                return carry

            lax.fori_loop(0, 4, fold, 0)
        for step in (1, 2, 3):
            for part, (ia, along_a, ib, along_b) in enumerate(self.ways):
                to = lax.rem(ib + step, 4)
                self.flying.append(
                    self.go(a1.at[:, part, to], self.r2.at[part, step - 1], along_b(step))
                )

    def step3(self):
        self.wait()
        a1, r2, a2, r3, mp, x_hi = self.a1, self.r2, self.a2, self.r3, self.mp, self.x_hi
        for part, (ia, along_a, ib, along_b) in enumerate(self.ways):
            total = a1[:, part, ib].astype(F32)
            for k in range(3):
                total = total + r2[part, k].astype(F32)
            a2[:, part] = total.astype(BF)
        self.flying = [
            self.go(a2.at[1 - mp, :, x_hi], r3.at[0], self.near),
            self.go(a2.at[1 - mp, :, 1 - x_hi], r3.at[1], self.far),
            self.go(a2.at[mp, :, 1 - x_hi], r3.at[2], self.opposite),
        ]

    def step4(self):
        self.wait()
        total = self.a2[self.mp, :, self.x_hi].astype(F32)
        for k in range(3):
            total = total + self.r3[k].astype(F32)
        total = total.astype(BF)
        for part, (ia, along_a, ib, along_b) in enumerate(self.ways):
            self.f[self.core, part, ia, ib, self.x_hi] = total[part]
        for part, (ia, along_a, ib, along_b) in enumerate(self.ways):
            spot = self.f.at[self.core, part, ia, ib, self.x_hi]
            self.flying.append(self.go(spot, spot, self.opposite))

    def step5(self):
        self.wait()
        for step in (1, 2, 3):
            for part, (ia, along_a, ib, along_b) in enumerate(self.ways):
                spot = self.f.at[self.core, part, ia, ib]
                self.flying.append(self.go(spot, spot, along_b(step)))

    def step6(self):
        self.wait()
        for step in (1, 2, 3):
            for part, (ia, along_a, ib, along_b) in enumerate(self.ways):
                spot = self.f.at[self.core, part, ia]
                self.flying.append(self.go(spot, spot, along_a(step)))

    def step7(self):
        self.wait()
        spot = self.f.at[self.core]
        self.flying = [self.go(spot, spot, self.sibling)]


def around(lat, lon, mp, step):
    row_lat, row_mp = row_step(lat, mp, step)
    col = lax.rem(lon + step + 8, 8)
    return (row_lat, lon, row_mp), (lat, col, mp), (row_lat, col, row_mp)


SENDS = 112
NEAR_ROWS = (96, 256)


def pair_kernel(
    fc, cc, wqp, wop, wqs, wos,
    ro, gfo, f_plain, f_shift,
    x, hx, cx, rs, rp, gs, gp, gf,
    fqp, fop, fqs, fos,
    n_p, pr_p, es_p, rd_p, mix_p,
    n_s, pr_s, es_s, rd_s, mix_s,
    cw, do, dpr,
    g_plain, g_shift,
    *rest,
):
    sums, (send, recv, local) = rest[:14], rest[14:]
    lat, lon, mp = place()
    row_prev, col_prev, corner_prev = around(lat, lon, mp, -1)
    row_next, col_next, corner_next = around(lat, lon, mp, 1)
    go = Sender(send, recv)
    sum_plain = Sum(go, g_plain, f_plain, *sums[:7])
    sum_shift = Sum(go, g_shift, f_shift, *sums[7:])
    near, far, sibling, core = sum_plain.near, sum_plain.far, sum_plain.sibling, sum_plain.core
    barrier(
        sum_plain.peers
        + [row_prev, col_prev, corner_prev, row_next, col_next, corner_next]
    )
    lanes = pl.ds(pl.multiple_of(mp * 256, 256), 256)
    away = pl.ds(pl.multiple_of((1 - mp) * 256, 256), 256)
    other_rows = pl.ds((1 - mp) * 4, 4)
    own_rows = pl.ds(mp * 4, 4)
    own = pl.ds(0, 4)
    kept = []

    def keep(src, dst):
        copy = pltpu.make_async_copy(src, dst, local.at[len(kept)])
        copy.start()
        kept.append(copy)
        return copy

    def weight(src, dst, split):
        parts = []
        for k, (base, size) in enumerate(((0, split // 2), (split, (512 - split) // 2))):
            rows = pl.ds(pl.multiple_of(base + core * size, 16), size)
            copy = go(src.at[:, rows], dst.at[:, rows, lanes], (near, far)[k])
            parts.append((copy, dst.at[:, rows, away]))
        return parts

    def weight_out(src, dst):
        rows = pl.ds(pl.multiple_of(core * 128, 128), 128)
        there = pl.ds(pl.multiple_of(mp * 256 + core * 128, 128), 128)
        here = pl.ds(pl.multiple_of((1 - mp) * 256 + core * 128, 128), 128)
        return [(go(src.at[rows], dst.at[there], far), dst.at[here])]

    def pass_on(parts):
        shared = []
        for copy, spot in parts:
            copy.wait_recv()
            shared.append(go(spot, spot, sibling))
        return shared

    fields_copy = go(fc.at[other_rows], x.at[:, :, :, lanes], near)
    qkv_p = weight(wqp, fqp, NEAR_ROWS[0])
    out_p = weight_out(wop, fop)
    cot_copy = go(cc.at[other_rows], cx.at[own, own, :, lanes], near)
    qkv_s = weight(wqs, fqs, NEAR_ROWS[1])
    out_s = weight_out(wos, fos)
    mp_rows = pl.ds(pl.multiple_of(mp * 256, 256), 256)
    x_kept = keep(fc.at[own_rows], x.at[:, :, :, lanes])
    wq_kept = keep(wqp, fqp.at[:, :, lanes])
    others = [
        keep(wop, fop.at[mp_rows]),
        keep(cc.at[own_rows], cx.at[own, own, :, lanes]),
        keep(wqs, fqs.at[:, :, lanes]),
        keep(wos, fos.at[mp_rows]),
    ]

    fields_copy.wait()
    x_kept.wait()
    forward_norm(x, 0, n_p, 0, 4)
    shared = pass_on(qkv_p)
    wq_kept.wait()
    for copy in shared:
        copy.wait_recv()
    forward_project(n_p, fqp, pr_p, 0, 4)
    shared_out = pass_on(out_p)
    forward_attend(pr_p, es_p, rd_p, mix_p, None, 0, 4)
    for copy in others:
        copy.wait()
    for copy in shared_out:
        copy.wait_recv()
    forward_out(x, 0, fop, mix_p, hx, 0, 4)

    halos = [
        go(hx.at[0, own], hx.at[4, own], row_prev),
        go(hx.at[own, 0], hx.at[own, 4], col_prev),
        go(hx.at[0, 0], hx.at[4, 4], corner_prev),
    ]
    cot_copy.wait()
    cot_halos = [
        go(cx.at[0, own], cx.at[4, own], row_prev),
        go(cx.at[own, 0], cx.at[own, 4], col_prev),
        go(cx.at[0, 0], cx.at[4, 4], corner_prev),
    ]
    shared_s = pass_on(qkv_s)
    forward_norm(hx, 1, n_s, 0, 1)
    for copy in shared_s:
        copy.wait_recv()
    cut = (lat * 2 + mp) == 15
    forward_project(n_s, fqs, pr_s, 0, 1)
    shared_out_s = pass_on(out_s)
    forward_attend(pr_s, es_s, rd_s, mix_s, cut, 0, 1)
    for copy in halos:
        copy.wait()
    forward_norm(hx, 1, n_s, 1, 4)
    forward_project(n_s, fqs, pr_s, 1, 4)
    forward_attend(pr_s, es_s, rd_s, mix_s, cut, 1, 4)
    for copy in shared_out_s:
        copy.wait_recv()
    forward_out(hx, 1, fos, mix_s, rs, 0, 4)

    low, high = pl.ds(0, 3), pl.ds(1, 3)

    def narrow(src, dst):
        return [
            go(src.at[3, low], dst.at[0, high], row_next),
            go(src.at[low, 3], dst.at[high, 0], col_next),
            go(src.at[3, 3], dst.at[0, 0], corner_next),
            keep(src.at[low, low], dst.at[high, high]),
        ]

    result_halos = narrow(rs, rp)

    for copy in cot_halos:
        copy.wait()
    backward_out(cx, 1, fos, mix_s, cw, do, g_shift)
    backward_attend(pr_s, es_s, rd_s, mix_s, do, dpr, 0, 4)
    backward_tokens(hx, 1, fqs, cw, dpr, gs)
    grad_halos = narrow(gs, gp)
    for copy in result_halos:
        copy.wait()
    ends = [go(rp.at[:, :, :, away], ro.at[own_rows], near)]
    ends.append(keep(rp.at[:, :, :, lanes], ro.at[own_rows]))
    backward_weights(n_s, dpr, g_shift)
    sum_shift.step0()

    for copy in grad_halos:
        copy.wait()
    backward_out(gp, 0, fop, mix_p, cw, do, g_plain)
    sum_shift.step1()
    backward_attend(pr_p, es_p, rd_p, mix_p, do, dpr, 0, 2)
    sum_shift.step2()
    backward_attend(pr_p, es_p, rd_p, mix_p, do, dpr, 2, 4)
    sum_shift.step3()
    backward_weights(n_p, dpr, g_plain)
    sum_plain.step0()
    sum_shift.step4()
    backward_tokens(x, 0, fqp, cw, dpr, gf)
    ends.append(go(gf.at[:, :, :, away], gfo.at[own_rows], near))
    ends.append(keep(gf.at[:, :, :, lanes], gfo.at[own_rows]))
    sum_plain.step1()
    sum_shift.step5()
    sum_plain.step2()
    sum_shift.step6()
    sum_plain.step3()
    sum_plain.step4()
    sum_shift.step7()
    sum_plain.step5()
    sum_plain.step6()
    sum_plain.step7()
    sum_shift.wait()
    sum_plain.wait()
    for copy in ends:
        copy.wait()
    for copy, _ in qkv_p + out_p + qkv_s + out_s:
        copy.wait_send()
    for copy in shared + shared_out + shared_s + shared_out_s:
        copy.wait_send()


def shape(*dims, dtype=BF):
    return jax.ShapeDtypeStruct(dims, dtype)


GRID = (4, 4, 32, 512)
WIDE = (5, 5, 32, 512)
HELD = (8, 4, 32, 256)
SAVED = (
    ((4, 128, 512), BF),
    ((4, 128, 1536), BF),
    ((4, 4, 128, 512), BF),
    ((4, 128, 512), F32),
    ((4, 128, 512), BF),
)
SUM = (
    (2, 2, 4, 4, 2, 16, 256),
    (2, 2, 4, 4, 2, 16, 256),
    (2, 3, 2, 4, 2, 16, 256),
    (2, 2, 4, 2, 16, 256),
    (2, 3, 2, 2, 16, 256),
    (2, 2, 2, 16, 256),
    (3, 2, 16, 256),
)
SCRATCH = (
    [(s, BF) for s in (GRID, WIDE, WIDE, GRID, GRID, GRID, GRID, GRID)]
    + [((3, 512, 512), BF), ((512, 512), BF)] * 2
    + list(SAVED) * 2
    + [((4, 128, 512), BF), ((4, 128, 512), F32), ((4, 128, 1536), BF)]
    + [((2, 2, 2, 4, 4, 2, 16, 256), BF)] * 2
    + [(s, BF) for s in SUM] * 2
)


def cells(tokens):
    return tokens.reshape(8, 4, 4, 8, 256).transpose(0, 2, 1, 3, 4).reshape(8, 4, 32, 256)


def uncells(tokens):
    return tokens.reshape(8, 4, 4, 8, 256).transpose(0, 2, 1, 3, 4).reshape(32, 32, 256)


def on_device(fields, qkv_plain, out_plain, qkv_shift, out_shift, cotangent):
    factor = (fields.shape[0] * fields.shape[1] * 64) ** -0.5
    vmem = pl.BlockSpec(memory_space=pltpu.VMEM)
    hbm = pl.BlockSpec(memory_space=pl.ANY)
    f_shape = (2, 2, 4, 4, 2, 16, 256)
    result, grad_fields, f_plain, f_shift = pl.pallas_call(
        pair_kernel,
        out_shape=[shape(*HELD), shape(*HELD), shape(*f_shape), shape(*f_shape)],
        in_specs=[hbm] * 6,
        out_specs=[vmem] * 4,
        scratch_shapes=[pltpu.VMEM(s, t) for s, t in SCRATCH]
        + [
            pltpu.SemaphoreType.DMA((SENDS,)),
            pltpu.SemaphoreType.DMA((SENDS,)),
            pltpu.SemaphoreType.DMA((10,)),
        ],
        compiler_params=pltpu.CompilerParams(
            collective_id=0, has_side_effects=True, vmem_limit_bytes=VMEM_LIMIT
        ),
    )(
        cells(fields),
        cells(cotangent),
        qkv_plain.transpose(1, 0, 2),
        out_plain,
        qkv_shift.transpose(1, 0, 2),
        out_shift,
    )
    outs = []
    for summed in (f_plain, f_shift):
        summed = summed.reshape(2048, 256).astype(F32) * factor
        outs.append(summed[:1536].reshape(3, 512, 256).transpose(1, 0, 2))
        outs.append(jnp.concatenate([summed[1536:1792], summed[1792:]], 1))
    return (uncells(result), uncells(grad_fields), *outs)


def solution(mesh):
    in_specs = (
        P("lat", "lon", "mp"),
        P(None, None, "mp"),
        P("mp", None),
        P(None, None, "mp"),
        P("mp", None),
        P("lat", "lon", "mp"),
    )
    out_specs = (
        P("lat", "lon", "mp"),
        P("lat", "lon", "mp"),
        P(None, None, "mp"),
        P("mp", None),
        P(None, None, "mp"),
        P("mp", None),
    )
    return jax.shard_map(
        on_device, mesh=mesh, in_specs=in_specs, out_specs=out_specs, check_vma=False
    )
```

```python
import functools

import jax
import jax.numpy as jnp
from jax import lax
from jax.experimental import pallas as pl
from jax.experimental.pallas import tpu as pltpu
from jax.sharding import PartitionSpec as P

BF = jnp.bfloat16
F32 = jnp.float32
MESH = pl.DeviceIdType.MESH
VMEM_LIMIT = 56 * 1024 * 1024
D = 512
HEAD_DIM = 32
SCALE = HEAD_DIM ** -0.5
LOG2E = 1.4426950408889634


def place():
    lat, lon, mp = lax.axis_index("lat"), lax.axis_index("lon"), lax.axis_index("mp")
    return lat, lon, mp


def row_step(lat, mp, step):
    at = lax.rem(lat * 2 + mp + step + 16, 16)
    return at // 2, lax.rem(at, 2)


def barrier(peers):
    sem = pltpu.get_barrier_semaphore()
    for peer in peers:
        pl.semaphore_signal(sem, inc=1, device_id=peer, device_id_type=MESH)
    pl.semaphore_wait(sem, len(peers))


class Sender:
    def __init__(self, send, recv):
        self.send, self.recv, self.used = send, recv, 0

    def __call__(self, src, dst, peer):
        copy = pltpu.make_async_remote_copy(
            src_ref=src,
            dst_ref=dst,
            send_sem=self.send.at[self.used],
            recv_sem=self.recv.at[self.used],
            device_id=peer,
            device_id_type=MESH,
        )
        self.used += 1
        copy.start()
        return copy


NN = (((1,), (0,)), ((), ()))
NT = (((1,), (1,)), ((), ()))
TN = (((0,), (0,)), ((), ()))


def dot(left, right, dims=NN):
    return lax.dot_general(left, right, dims, preferred_element_type=F32)


def head_masks():
    lane = lax.broadcasted_iota(jnp.int32, (128, 128), 1) // HEAD_DIM
    return [lane == h for h in range(4)]


def spread_heads(block, masks):
    zero = jnp.zeros_like(block)
    return jnp.concatenate([jnp.where(m, block, zero) for m in masks], 0)


def merge_heads(tall, masks):
    total = jnp.where(masks[0], tall[0:128], 0.0)
    for h in range(1, 4):
        total = jnp.where(masks[h], tall[h * 128 : (h + 1) * 128], total)
    return total


def standardize(x):
    centred = x - jnp.mean(x, -1, keepdims=True)
    inv = lax.rsqrt(jnp.mean(centred * centred, -1, keepdims=True) + 1e-05)
    return centred * inv, inv


def window(ref, w, offset):
    i, j = w // 2, lax.rem(w, 2)
    got = ref[pl.ds(2 * i + offset, 2), pl.ds(2 * j + offset, 2)]
    return got.reshape(128, D)


def put_window(ref, w, value):
    i, j = w // 2, lax.rem(w, 2)
    ref[pl.ds(2 * i, 2), pl.ds(2 * j, 2)] = value.reshape(2, 2, 32, D)


def rows_window(ref, w):
    i, j = w // 2, lax.rem(w, 2)
    got = ref[pl.ds(8 * i, 8), pl.ds(pl.multiple_of(16 * j, 16), 16)]
    return got.reshape(128, D)


def put_rows(ref, w, value):
    i, j = w // 2, lax.rem(w, 2)
    ref[pl.ds(8 * i, 8), pl.ds(pl.multiple_of(16 * j, 16), 16)] = value.reshape(8, 16, D)


def cells_of(value):
    return value.reshape(2, 4, 2, 8, D).transpose(0, 2, 1, 3, 4).reshape(128, D)


def rows_of(value):
    return value.reshape(2, 2, 4, 8, D).transpose(0, 2, 1, 3, 4).reshape(128, D)


def forward_norm(take, n, low, high):
    def norm(w, carry):
        n[w] = standardize(take(w).astype(F32))[0].astype(BF)
        return carry

    lax.fori_loop(low, high, norm, 0)


def forward_project(n, wq, pr, low, high, kinds=(0, 1, 2)):
    count = high - low
    for c in kinds:
        for j in range(2):
            cols = slice(c * 512 + j * 256, c * 512 + (j + 1) * 256)
            got = dot(n[low:high].reshape(count * 128, 512), wq[c, :, j * 256 : (j + 1) * 256])
            pr[low:high, :, cols] = got.astype(BF).reshape(count, 128, 256)


def forward_attend(pr, es, rd, mix, cut, low, high):
    masks = head_masks()
    ones = spread_heads(jnp.ones((128, 128), BF), masks)
    if cut is not None:
        q_half = lax.broadcasted_iota(jnp.int32, (128, 512), 0) // 64
        k_half = lax.rem(lax.broadcasted_iota(jnp.int32, (128, 512), 1) // 64, 2)
        same = q_half == k_half

    def attend(w, carry):
        for s in range(4):
            q = pr[w, :, s * 128 : (s + 1) * 128]
            k = spread_heads(pr[w, :, 512 + s * 128 : 512 + (s + 1) * 128], masks)
            v = spread_heads(pr[w, :, 1024 + s * 128 : 1024 + (s + 1) * 128], masks)
            e = jnp.exp2(dot(q, k, NT) * (SCALE * LOG2E))
            if cut is not None:
                e = jnp.where(same | jnp.logical_not(cut & (w >= 2)), e, 0.0)
            e = e.astype(BF)
            es[w, s] = e
            both = dot(e, jnp.concatenate([v, ones], 1))
            inv = 1.0 / both[:, 128:]
            rd[w, :, s * 128 : (s + 1) * 128] = inv
            mix[w, :, s * 128 : (s + 1) * 128] = (both[:, :128] * inv).astype(BF)
        return carry

    lax.fori_loop(low, high, attend, 0)


def forward_out(take, wo, mix, put, work):
    work[...] = dot(mix[...].reshape(512, 512), wo[...]).reshape(4, 128, 512)

    def project(w, carry):
        put(w, take(w).astype(F32) + work[w])
        return carry

    lax.fori_loop(0, 4, project, 0)


def backward_do(take, wo, cw, do, low, high):
    count = high - low

    def gather(w, carry):
        cw[w] = take(w)
        return carry

    lax.fori_loop(low, high, gather, 0)
    for j in range(2):
        cols = slice(j * 256, (j + 1) * 256)
        got = dot(cw[low:high].reshape(count * 128, 512), wo[cols, :], NT)
        do[low:high, :, cols] = got.reshape(count, 128, 256)


def backward_out(mix, cw, g):
    for j in range(2):
        cols = slice(j * 256, (j + 1) * 256)
        got = dot(mix[:, :, cols].reshape(512, 256), cw[...].reshape(512, 512), TN).astype(BF)
        g[j, 1, 1, 0:2] = got[:, 0:256].reshape(2, 4, 2, 16, 256)
        g[j, 1, 1, 2:4] = got[:, 256:512].reshape(2, 4, 2, 16, 256)


def backward_attend(pr, es, rd, mix, do, dpr, low, high):
    masks = head_masks()
    ones = spread_heads(jnp.ones((128, 128), BF), masks)

    def attend(w, carry):
        for s in range(4):
            lanes = slice(s * 128, (s + 1) * 128)
            q = pr[w, :, lanes]
            k = spread_heads(pr[w, :, 512 + s * 128 : 512 + (s + 1) * 128], masks)
            v = spread_heads(pr[w, :, 1024 + s * 128 : 1024 + (s + 1) * 128], masks)
            e = es[w, s]
            g1 = do[w, :, lanes] * rd[w, :, lanes]
            g2 = g1 * mix[w, :, lanes].astype(F32)
            g1 = g1.astype(BF)
            t = dot(jnp.concatenate([g1, (-g2).astype(BF)], 1), jnp.concatenate([v, ones], 1), NT)
            ds = (e.astype(F32) * t).astype(BF)
            dq = dot(ds, k) * SCALE
            dk = merge_heads(dot(ds, q, TN), masks) * SCALE
            dv = merge_heads(dot(e, g1, TN), masks)
            dpr[w, :, lanes] = dq.astype(BF)
            dpr[w, :, 512 + s * 128 : 512 + (s + 1) * 128] = dk.astype(BF)
            dpr[w, :, 1024 + s * 128 : 1024 + (s + 1) * 128] = dv.astype(BF)
        return carry

    lax.fori_loop(low, high, attend, 0)


def backward_weights(n, dpr, g):
    for c in range(3):
        for j in range(2):
            cols = slice(c * 512 + j * 256, c * 512 + (j + 1) * 256)
            got = dot(n[...].reshape(512, 512), dpr[:, :, cols].reshape(512, 256), TN)
            g[j, c // 2, c % 2] = got.astype(BF).reshape(4, 4, 2, 16, 256)


def backward_tokens(take, wq, cw, dpr, put, work, low, high):
    count = high - low
    grad = dot(dpr[low:high, :, 0:512].reshape(count * 128, 512), wq[0], NT)
    for c in (1, 2):
        part = dpr[low:high, :, c * 512 : (c + 1) * 512].reshape(count * 128, 512)
        grad = grad + dot(part, wq[c], NT)
    work[low:high] = grad.reshape(count, 128, 512)

    def finish(w, carry):
        grad = work[w]
        standard, inv = standardize(take(w).astype(F32))
        back = inv * (
            grad
            - jnp.mean(grad, -1, keepdims=True)
            - standard * jnp.mean(grad * standard, -1, keepdims=True)
        )
        put(w, cw[w].astype(F32) + back)
        return carry

    lax.fori_loop(low, high, finish, 0)


class Sum:
    def __init__(self, go, g, f, r0, a0, r1, a1, r2, a2, r3):
        self.go, self.g, self.f = go, g, f
        self.r0, self.a0, self.r1, self.a1, self.r2, self.a2, self.r3 = r0, a0, r1, a1, r2, a2, r3
        lat, lon, mp = place()
        self.mp, self.core, z = mp, lax.rem(lon, 2), lon // 2
        y, self.x_hi = lax.rem(lat, 4), lat // 4
        self.near = (lat, lon, 1 - mp)
        self.far = (lax.rem(lat + 4, 8), lon, 1 - mp)
        self.opposite = (lax.rem(lat + 4, 8), lon, mp)
        self.sibling = (lat, lon + 1 - 2 * self.core, mp)

        def along_y(step):
            return (lat // 4 * 4 + lax.rem(y + step, 4), lon, mp)

        def along_z(step):
            return (lat, lax.rem(z + step, 4) * 2 + lax.rem(lon, 2), mp)

        self.ways = ((y, along_y, z, along_z), (z, along_z, y, along_y))
        self.peers = [self.near, self.far, self.opposite, self.sibling]
        self.peers += [along_y(s) for s in (1, 2, 3)] + [along_z(s) for s in (1, 2, 3)]
        self.flying = []

    def wait(self):
        for copy in self.flying:
            copy.wait()
        self.flying = []

    def step0(self):
        self.flying = [self.go(self.g.at[:, 1 - self.core], self.r0, self.sibling)]

    def step1(self):
        self.wait()
        g, r0, a0, core = self.g, self.r0, self.a0, self.core

        def fold(n, carry):
            part, a = n // 4, lax.rem(n, 4)
            mine = g[:, core, part, a].astype(F32)
            a0[:, part, a] = (mine + r0[:, part, a].astype(F32)).astype(BF)
            return carry

        lax.fori_loop(0, 8, fold, 0)
        for step in (1, 2, 3):
            for part, (ia, along_a, ib, along_b) in enumerate(self.ways):
                to = lax.rem(ia + step, 4)
                self.flying.append(
                    self.go(a0.at[:, part, to], self.r1.at[part, step - 1], along_a(step))
                )

    def step2(self):
        self.wait()
        a0, r1, a1 = self.a0, self.r1, self.a1
        for part, (ia, along_a, ib, along_b) in enumerate(self.ways):

            def fold(b, carry):
                total = a0[:, part, ia, b].astype(F32)
                for k in range(3):
                    total = total + r1[part, k, :, b].astype(F32)
                a1[:, part, b] = total.astype(BF)
                return carry

            lax.fori_loop(0, 4, fold, 0)
        for step in (1, 2, 3):
            for part, (ia, along_a, ib, along_b) in enumerate(self.ways):
                to = lax.rem(ib + step, 4)
                self.flying.append(
                    self.go(a1.at[:, part, to], self.r2.at[part, step - 1], along_b(step))
                )

    def step3(self):
        self.wait()
        a1, r2, a2, r3, mp = self.a1, self.r2, self.a2, self.r3, self.mp
        for part, (ia, along_a, ib, along_b) in enumerate(self.ways):
            total = a1[:, part, ib].astype(F32)
            for k in range(3):
                total = total + r2[part, k].astype(F32)
            a2[:, part] = total.astype(BF)
        self.flying = [
            self.go(a2.at[1 - mp], r3.at[0], self.near),
            self.go(a2.at[1 - mp], r3.at[1], self.far),
            self.go(a2.at[mp], r3.at[2], self.opposite),
        ]

    def step4(self):
        self.wait()
        same = self.a2[self.mp].astype(F32) + self.r3[2].astype(F32)
        other = self.r3[0].astype(F32) + self.r3[1].astype(F32)
        total = (same + other).astype(BF)
        for part, (ia, along_a, ib, along_b) in enumerate(self.ways):
            self.f[self.core, part, ia, ib] = total[part]
        for step in (1, 2, 3):
            for part, (ia, along_a, ib, along_b) in enumerate(self.ways):
                spot = self.f.at[self.core, part, ia, ib]
                self.flying.append(self.go(spot, spot, along_b(step)))

    def step5(self):
        self.wait()
        self.coming = []
        for step in (1, 2, 3):
            for part, (ia, along_a, ib, along_b) in enumerate(self.ways):
                spot = self.f.at[self.core, part, ia]
                arrives = self.f.at[self.core, part, lax.rem(ia + 4 - step, 4)]
                self.coming.append((self.go(spot, spot, along_a(step)), arrives))
        for part, (ia, along_a, ib, along_b) in enumerate(self.ways):
            spot = self.f.at[self.core, part, ia]
            self.flying.append(self.go(spot, spot, self.sibling))

    def step6(self):
        for copy, spot in self.coming:
            copy.wait_recv()
            self.flying.append(self.go(spot, spot, self.sibling))

    def last(self):
        self.wait()
        for copy, _ in self.coming:
            copy.wait_send()


def around(lat, lon, mp, step):
    row_lat, row_mp = row_step(lat, mp, step)
    col = lax.rem(lon + step + 8, 8)
    return (row_lat, lon, row_mp), (lat, col, mp), (row_lat, col, row_mp)


SENDS = 112


def pair_kernel(
    fc, cc, wqp, wop, wqs, wos,
    ro, gfo, f_plain, f_shift,
    x, hx, cx, rs, rp, gs, gp, gf, rn,
    fqp, fop, fqs, fos,
    n_p, pr_p, es_p, rd_p, mix_p,
    n_s, pr_s, es_s, rd_s, mix_s,
    cw, do, dpr, cn,
    g_plain, g_shift,
    *rest,
):
    sums, (send, recv, local) = rest[:14], rest[14:]
    lat, lon, mp = place()
    row_prev, col_prev, corner_prev = around(lat, lon, mp, -1)
    row_next, col_next, corner_next = around(lat, lon, mp, 1)
    go = Sender(send, recv)
    sum_plain = Sum(go, g_plain, f_plain, *sums[:7])
    sum_shift = Sum(go, g_shift, f_shift, *sums[7:])
    near, far, sibling, core = sum_plain.near, sum_plain.far, sum_plain.sibling, sum_plain.core
    barrier(
        sum_plain.peers
        + [row_prev, col_prev, corner_prev, row_next, col_next, corner_next]
    )
    lanes = pl.ds(pl.multiple_of(mp * 256, 256), 256)
    away = pl.ds(pl.multiple_of((1 - mp) * 256, 256), 256)
    other_rows = pl.ds((1 - mp) * 16, 16)
    own_rows = pl.ds(mp * 16, 16)
    own = pl.ds(0, 4)
    kept = []

    def keep(src, dst):
        copy = pltpu.make_async_copy(src, dst, local.at[len(kept)])
        copy.start()
        kept.append(copy)
        return copy

    def weight(src, dst, c, peer):
        rows = pl.ds(pl.multiple_of(core * 256, 256), 256)
        return go(src.at[c, rows], dst.at[c, rows, lanes], peer), dst.at[c, rows, away]

    def weight_out(src, dst, peer):
        rows = pl.ds(pl.multiple_of(core * 128, 128), 128)
        there = pl.ds(pl.multiple_of(mp * 256 + core * 128, 128), 128)
        here = pl.ds(pl.multiple_of((1 - mp) * 256 + core * 128, 128), 128)
        return go(src.at[rows], dst.at[there], peer), dst.at[here]

    y, z = lax.rem(lat, 4), lon // 2
    along_y, along_z = sum_plain.ways[0][1], sum_plain.ways[0][3]
    rows_s = pl.ds(pl.multiple_of(core * 256 + y * 64, 64), 64)
    half_s = pl.ds(pl.multiple_of(core * 256, 256), 256)
    at_o = core * 128 + z * 32
    rows_o = pl.ds(pl.multiple_of(at_o, 32), 32)
    there_o = pl.ds(pl.multiple_of(mp * 256 + at_o, 32), 32)
    here_o = pl.ds(pl.multiple_of((1 - mp) * 256 + at_o, 32), 32)
    half_o = pl.ds(pl.multiple_of((1 - mp) * 256 + core * 128, 128), 128)

    unsent = []

    def pass_on(part):
        copy, spot = part
        copy.wait_recv()
        unsent.append(copy)
        passed = go(spot, spot, sibling)
        unsent.append(passed)
        return passed

    fields_copy = go(fc.at[other_rows], x.at[:, :, lanes], near)
    qkv_p = [weight(wqp, fqp, c, far) for c in range(3)]
    x_kept = keep(fc.at[own_rows], x.at[:, :, lanes])
    mp_rows = pl.ds(pl.multiple_of(mp * 256, 256), 256)
    others = [
        keep(wqp, fqp.at[:, :, lanes]),
        keep(wop, fop.at[mp_rows]),
        keep(wqs, fqs.at[:, :, lanes]),
        keep(wos, fos.at[mp_rows]),
        keep(cc.at[own_rows], cn.at[:, :, lanes]),
    ]

    def take_x(w):
        return rows_window(x, w)

    def put_hidden(w, value):
        put_window(hx, w, cells_of(value).astype(BF))

    fields_copy.wait()
    x_kept.wait()
    over_x = [
        go(wqs.at[:, rows_s], fqs.at[:, rows_s, lanes], near),
        go(wos.at[rows_o], fos.at[there_o], near),
    ]
    forward_norm(take_x, n_p, 0, 4)
    for copy in others:
        copy.wait()
    passed = pass_on(qkv_p[0])
    for c in range(3):
        passed_next = pass_on(qkv_p[c + 1]) if c < 2 else None
        passed.wait_recv()
        if c == 2:
            out_p = weight_out(wop, fop, far)
        forward_project(n_p, fqp, pr_p, 0, 4, (c,))
        passed = passed_next
    for copy in over_x:
        copy.wait_recv()
    unsent.extend(over_x)
    spread = []
    for step in (1, 2, 3):
        spot = fqs.at[:, rows_s, away]
        spread.append(go(spot, spot, along_y(step)))
        spot = fos.at[here_o]
        spread.append(go(spot, spot, along_z(step)))
    cot_copy = go(cc.at[other_rows], cn.at[:, :, lanes], near)
    forward_attend(pr_p, es_p, rd_p, mix_p, None, 0, 4)
    pass_on(out_p).wait_recv()
    forward_out(take_x, fop, mix_p, put_hidden, do)

    halos = [
        go(hx.at[0, own], hx.at[4, own], row_prev),
        go(hx.at[own, 0], hx.at[own, 4], col_prev),
        go(hx.at[0, 0], hx.at[4, 4], corner_prev),
    ]

    def take_hidden(w):
        return window(hx, w, 1)

    for copy in spread:
        copy.wait()
    spot = fqs.at[:, half_s, away]
    passed_qkv = go(spot, spot, sibling)
    spot = fos.at[half_o]
    passed_out = go(spot, spot, sibling)
    forward_norm(take_hidden, n_s, 0, 1)
    passed_qkv.wait()
    forward_project(n_s, fqs, pr_s, 0, 1)
    cut = (lat * 2 + mp) == 15
    forward_attend(pr_s, es_s, rd_s, mix_s, cut, 0, 1)

    cot_copy.wait()

    def into_cells(w, carry):
        put_window(cx, w, cells_of(rows_window(cn, w).astype(F32)).astype(BF))
        return carry

    lax.fori_loop(0, 4, into_cells, 0)
    for copy in halos:
        copy.wait()
    cot_halos = [
        go(cx.at[0, own], cx.at[4, own], row_prev),
        go(cx.at[own, 0], cx.at[own, 4], col_prev),
        go(cx.at[0, 0], cx.at[4, 4], corner_prev),
    ]
    forward_norm(take_hidden, n_s, 1, 4)
    forward_project(n_s, fqs, pr_s, 1, 4)
    forward_attend(pr_s, es_s, rd_s, mix_s, cut, 1, 4)
    passed_out.wait()

    def put_result(w, value):
        put_window(rs, w, value.astype(BF))

    forward_out(take_hidden, fos, mix_s, put_result, do)

    low, high = pl.ds(0, 3), pl.ds(1, 3)

    def narrow(src, dst):
        return [
            go(src.at[3, low], dst.at[0, high], row_next),
            go(src.at[low, 3], dst.at[high, 0], col_next),
            go(src.at[3, 3], dst.at[0, 0], corner_next),
            keep(src.at[low, low], dst.at[high, high]),
        ]

    result_halos = narrow(rs, rp)

    def take_cot(w):
        return window(cx, w, 1)

    def put_grad(w, value):
        put_window(gs, w, value.astype(BF))

    for copy in cot_halos:
        copy.wait()
    backward_do(take_cot, fos, cw, do, 0, 4)
    backward_out(mix_s, cw, g_shift)
    backward_attend(pr_s, es_s, rd_s, mix_s, do, dpr, 0, 4)
    backward_tokens(take_hidden, fqs, cw, dpr, put_grad, do, 0, 4)
    grad_halos = narrow(gs, gp)
    backward_weights(n_s, dpr, g_shift)
    sum_shift.step0()
    for copy in result_halos:
        copy.wait()

    def into_rows(w, carry):
        put_rows(rn, w, rows_of(window(rp, w, 0).astype(F32)).astype(BF))
        return carry

    lax.fori_loop(0, 4, into_rows, 0)
    ends = [go(rn.at[:, :, away], ro.at[own_rows], near)]
    ends.append(keep(rn.at[:, :, lanes], ro.at[own_rows]))

    def take_back(w):
        return rows_of(window(gp, w, 0).astype(F32)).astype(BF)

    def put_fields(w, value):
        put_rows(gf, w, value.astype(BF))

    grad_halos.pop().wait()
    backward_do(take_back, fop, cw, do, 3, 4)
    backward_attend(pr_p, es_p, rd_p, mix_p, do, dpr, 3, 4)
    for copy in grad_halos:
        copy.wait()
    backward_do(take_back, fop, cw, do, 0, 3)
    backward_out(mix_p, cw, g_plain)
    sum_shift.step1()
    backward_attend(pr_p, es_p, rd_p, mix_p, do, dpr, 0, 3)
    sum_shift.step2()
    backward_weights(n_p, dpr, g_plain)
    sum_plain.step0()
    for half in range(2):
        backward_tokens(take_x, fqp, cw, dpr, put_fields, do, half * 2, half * 2 + 2)
        rows = pl.ds(half * 8, 8)
        there = pl.ds(mp * 16 + half * 8, 8)
        ends.append(go(gf.at[rows, :, away], gfo.at[there], near))
        ends.append(keep(gf.at[rows, :, lanes], gfo.at[there]))
        if half == 0:
            sum_plain.step1()
            sum_shift.step3()
    sum_shift.step4()
    sum_plain.step2()
    sum_shift.step5()
    sum_plain.step3()
    sum_shift.step6()
    sum_plain.step4()
    sum_plain.step5()
    sum_plain.step6()
    sum_shift.last()
    sum_plain.last()
    for copy in ends:
        copy.wait()
    for copy in unsent:
        copy.wait_send()


def last_kernel(
    factor, f_plain, f_shift, r, gf, qkv_p, out_p, qkv_s, out_s, ro, gfo, raw, wide, held, came, gone
):
    coming, going = [], []

    def move(src, dst, sem, to):
        copy = pltpu.make_async_copy(src, dst, sem)
        copy.start()
        to.append(copy)

    for n in range(8):
        rows = pl.ds(n % 4 * 512, 512)
        move((f_plain, f_shift)[n // 4].at[rows], raw.at[n], came.at[n], coming)
    for n, src in enumerate((r, gf)):
        move(src, held.at[n], came.at[8 + n], coming)
    for n in range(8):
        coming[n].wait()
        wide[n] = raw[n].astype(F32) * factor
        if n % 4 < 3:
            move(wide.at[n], (qkv_p, qkv_s)[n // 4].at[n % 4], gone.at[n], going)
        else:
            for k in range(2):
                cols = pl.ds(k * 256, 256)
                dst = (out_p, out_s)[n // 4].at[:, cols]
                move(wide.at[n, cols], dst, gone.at[8 + n // 4 * 2 + k], going)
    for n, dst in enumerate((ro, gfo)):
        coming[8 + n].wait()
        move(held.at[n], dst, gone.at[12 + n], going)
    for copy in going:
        copy.wait()


def shape(*dims, dtype=BF):
    return jax.ShapeDtypeStruct(dims, dtype)


GRID = (4, 4, 32, 512)
WIDE = (5, 5, 32, 512)
ROWS = (16, 32, 512)
HELD = (32, 32, 256)
SAVED = (
    ((4, 128, 512), BF),
    ((4, 128, 1536), BF),
    ((4, 4, 128, 512), BF),
    ((4, 128, 512), F32),
    ((4, 128, 512), BF),
)
SUM = (
    (2, 2, 4, 4, 2, 16, 256),
    (2, 2, 4, 4, 2, 16, 256),
    (2, 3, 2, 4, 2, 16, 256),
    (2, 2, 4, 2, 16, 256),
    (2, 3, 2, 2, 16, 256),
    (2, 2, 2, 16, 256),
    (3, 2, 2, 16, 256),
)
SCRATCH = (
    [(s, BF) for s in (ROWS, WIDE, WIDE, GRID, GRID, GRID, GRID, ROWS, ROWS)]
    + [((3, 512, 512), BF), ((512, 512), BF)] * 2
    + list(SAVED) * 2
    + [((4, 128, 512), BF), ((4, 128, 512), F32), ((4, 128, 1536), BF), (ROWS, BF)]
    + [((2, 2, 2, 4, 4, 2, 16, 256), BF)] * 2
    + [(s, BF) for s in SUM] * 2
)


def on_device(fields, qkv_plain, out_plain, qkv_shift, out_shift, cotangent):
    factor = (fields.shape[0] * fields.shape[1] * 64) ** -0.5
    vmem = pl.BlockSpec(memory_space=pltpu.VMEM)
    hbm = pl.BlockSpec(memory_space=pl.ANY)
    f_shape = (2, 2, 4, 4, 2, 16, 256)
    result, grad_fields, f_plain, f_shift = pl.pallas_call(
        pair_kernel,
        out_shape=[shape(*HELD), shape(*HELD), shape(*f_shape), shape(*f_shape)],
        in_specs=[hbm] * 6,
        out_specs=[vmem] * 4,
        scratch_shapes=[pltpu.VMEM(s, t) for s, t in SCRATCH]
        + [
            pltpu.SemaphoreType.DMA((SENDS,)),
            pltpu.SemaphoreType.DMA((SENDS,)),
            pltpu.SemaphoreType.DMA((12,)),
        ],
        compiler_params=pltpu.CompilerParams(
            collective_id=0, has_side_effects=True, vmem_limit_bytes=VMEM_LIMIT
        ),
    )(
        fields,
        cotangent,
        qkv_plain.transpose(1, 0, 2),
        out_plain,
        qkv_shift.transpose(1, 0, 2),
        out_shift,
    )
    qkv, out = shape(3, 512, 256, dtype=F32), shape(256, 512, dtype=F32)
    qkv_p, out_p, qkv_s, out_s, result, grad_fields = pl.pallas_call(
        functools.partial(last_kernel, factor),
        out_shape=[qkv, out, qkv, out, shape(*HELD), shape(*HELD)],
        in_specs=[hbm] * 4,
        out_specs=[hbm] * 6,
        scratch_shapes=[
            pltpu.VMEM((8, 512, 256), BF),
            pltpu.VMEM((8, 512, 256), F32),
            pltpu.VMEM((2,) + HELD, BF),
            pltpu.SemaphoreType.DMA((10,)),
            pltpu.SemaphoreType.DMA((14,)),
        ],
        compiler_params=pltpu.CompilerParams(vmem_limit_bytes=VMEM_LIMIT),
    )(f_plain.reshape(2048, 256), f_shift.reshape(2048, 256), result, grad_fields)
    return (
        result,
        grad_fields,
        qkv_p.transpose(1, 0, 2),
        out_p,
        qkv_s.transpose(1, 0, 2),
        out_s,
    )


def solution(mesh):
    in_specs = (
        P("lat", "lon", "mp"),
        P(None, None, "mp"),
        P("mp", None),
        P(None, None, "mp"),
        P("mp", None),
        P("lat", "lon", "mp"),
    )
    out_specs = (
        P("lat", "lon", "mp"),
        P("lat", "lon", "mp"),
        P(None, None, "mp"),
        P("mp", None),
        P(None, None, "mp"),
        P("mp", None),
    )
    return jax.shard_map(
        on_device, mesh=mesh, in_specs=in_specs, out_specs=out_specs, check_vma=False
    )
```

```python
import functools

import jax
import jax.numpy as jnp
from jax import lax
from jax.experimental import pallas as pl
from jax.experimental.pallas import tpu as pltpu
from jax.sharding import PartitionSpec as P

BF = jnp.bfloat16
F32 = jnp.float32
MESH = pl.DeviceIdType.MESH
VMEM_LIMIT = 56 * 1024 * 1024
D = 512
HEAD_DIM = 32
SCALE = HEAD_DIM ** -0.5
LOG2E = 1.4426950408889634


def place():
    lat, lon, mp = lax.axis_index("lat"), lax.axis_index("lon"), lax.axis_index("mp")
    return lat, lon, mp


def row_step(lat, mp, step):
    at = lax.rem(lat * 2 + mp + step + 16, 16)
    return at // 2, lax.rem(at, 2)


def barrier(peers):
    sem = pltpu.get_barrier_semaphore()
    for peer in peers:
        pl.semaphore_signal(sem, inc=1, device_id=peer, device_id_type=MESH)
    pl.semaphore_wait(sem, len(peers))


class Sender:
    def __init__(self, send, recv):
        self.send, self.recv, self.used = send, recv, 0

    def __call__(self, src, dst, peer):
        copy = pltpu.make_async_remote_copy(
            src_ref=src,
            dst_ref=dst,
            send_sem=self.send.at[self.used],
            recv_sem=self.recv.at[self.used],
            device_id=peer,
            device_id_type=MESH,
        )
        self.used += 1
        copy.start()
        return copy


NN = (((1,), (0,)), ((), ()))
NT = (((1,), (1,)), ((), ()))
TN = (((0,), (0,)), ((), ()))


def dot(left, right, dims=NN):
    return lax.dot_general(left, right, dims, preferred_element_type=F32)


def head_masks():
    lane = lax.broadcasted_iota(jnp.int32, (128, 128), 1) // HEAD_DIM
    return [lane == h for h in range(4)]


def spread_heads(block, masks):
    zero = jnp.zeros_like(block)
    return jnp.concatenate([jnp.where(m, block, zero) for m in masks], 0)


def merge_heads(tall, masks):
    total = jnp.where(masks[0], tall[0:128], 0.0)
    for h in range(1, 4):
        total = jnp.where(masks[h], tall[h * 128 : (h + 1) * 128], total)
    return total


def standardize(x):
    centred = x - jnp.mean(x, -1, keepdims=True)
    inv = lax.rsqrt(jnp.mean(centred * centred, -1, keepdims=True) + 1e-05)
    return centred * inv, inv


def window(ref, w, offset):
    i, j = w // 2, lax.rem(w, 2)
    got = ref[pl.ds(2 * i + offset, 2), pl.ds(2 * j + offset, 2)]
    return got.reshape(128, D)


def put_window(ref, w, value):
    i, j = w // 2, lax.rem(w, 2)
    ref[pl.ds(2 * i, 2), pl.ds(2 * j, 2)] = value.reshape(2, 2, 32, D)


def rows_window(ref, w):
    i, j = w // 2, lax.rem(w, 2)
    got = ref[pl.ds(8 * i, 8), pl.ds(pl.multiple_of(16 * j, 16), 16)]
    return got.reshape(128, D)


def put_rows(ref, w, value):
    i, j = w // 2, lax.rem(w, 2)
    ref[pl.ds(8 * i, 8), pl.ds(pl.multiple_of(16 * j, 16), 16)] = value.reshape(8, 16, D)


def cells_of(value):
    return value.reshape(2, 4, 2, 8, D).transpose(0, 2, 1, 3, 4).reshape(128, D)


def rows_of(value):
    return value.reshape(2, 2, 4, 8, D).transpose(0, 2, 1, 3, 4).reshape(128, D)


def forward_norm(take, n, low, high):
    def norm(w, carry):
        n[w] = standardize(take(w).astype(F32))[0].astype(BF)
        return carry

    lax.fori_loop(low, high, norm, 0)


def lanes_at(start, size):
    if isinstance(start, int):
        return slice(start, start + size)
    return pl.ds(pl.multiple_of(start, size), size)


def forward_project(n, wq, pr, low, high, groups=(0, 1)):
    count = high - low
    for j in groups:
        for c in range(3):
            weight = wq[c, :, lanes_at(j * 256, 256)]
            got = dot(n[low:high].reshape(count * 128, 512), weight)
            pr[low:high, :, lanes_at(c * 512 + j * 256, 256)] = got.astype(BF).reshape(count, 128, 256)


def forward_attend(pr, es, rd, mix, cut, low, high, chosen=(0, 1, 2, 3)):
    masks = head_masks()
    ones = spread_heads(jnp.ones((128, 128), BF), masks)
    if cut is not None:
        q_half = lax.broadcasted_iota(jnp.int32, (128, 512), 0) // 64
        k_half = lax.rem(lax.broadcasted_iota(jnp.int32, (128, 512), 1) // 64, 2)
        same = q_half == k_half

    def attend(w, carry):
        scores = []
        for s in chosen:
            q = pr[w, :, lanes_at(s * 128, 128)]
            k = spread_heads(pr[w, :, lanes_at(512 + s * 128, 128)], masks)
            scores.append(dot(q, k, NT))
        es_now = []
        for score in scores:
            e = jnp.exp2(score * (SCALE * LOG2E))
            if cut is not None:
                e = jnp.where(same | jnp.logical_not(cut & (w >= 2)), e, 0.0)
            es_now.append(e.astype(BF))
        both = []
        for s, e in zip(chosen, es_now):
            v = spread_heads(pr[w, :, lanes_at(1024 + s * 128, 128)], masks)
            both.append(dot(e, jnp.concatenate([v, ones], 1)))
        for s, e, pair in zip(chosen, es_now, both):
            es[w, s] = e
            inv = 1.0 / pair[:, 128:]
            rd[w, :, lanes_at(s * 128, 128)] = inv
            mix[w, :, lanes_at(s * 128, 128)] = (pair[:, :128] * inv).astype(BF)
        return carry

    lax.fori_loop(low, high, attend, 0)


def forward_out(take, wo, mix, put, work, low, high):
    count = high - low
    got = dot(mix[low:high].reshape(count * 128, 512), wo[...])
    work[low:high] = got.reshape(count, 128, 512)

    def project(w, carry):
        put(w, take(w).astype(F32) + work[w])
        return carry

    lax.fori_loop(low, high, project, 0)


def backward_do(take, wo, cw, do, low, high):
    count = high - low

    def gather(w, carry):
        cw[w] = take(w)
        return carry

    lax.fori_loop(low, high, gather, 0)
    for j in range(2):
        cols = slice(j * 256, (j + 1) * 256)
        got = dot(cw[low:high].reshape(count * 128, 512), wo[cols, :], NT)
        do[low:high, :, cols] = got.reshape(count, 128, 256)


def backward_out(mix, cw, put):
    for j in range(2):
        cols = slice(j * 256, (j + 1) * 256)
        got = dot(mix[:, :, cols].reshape(512, 256), cw[...].reshape(512, 512), TN).astype(BF)
        put(3, j, jnp.concatenate([got[:, 0:256], got[:, 256:512]], 0))


def backward_values(es, rd, do, ge, dpr, low, high):
    masks = head_masks()

    def attend(w, carry):
        sets = [slice(s * 128, (s + 1) * 128) for s in range(4)]
        g1 = [(do[w, :, lanes] * rd[w, :, lanes]).astype(BF) for lanes in sets]
        tall = [dot(es[w, s], g1[s], TN) for s in range(4)]
        for s in range(4):
            ge[w, :, sets[s]] = g1[s]
            dv = merge_heads(tall[s], masks)
            dpr[w, :, 1024 + s * 128 : 1024 + (s + 1) * 128] = dv.astype(BF)
        return carry

    lax.fori_loop(low, high, attend, 0)


def backward_scores(pr, es, mix, ge, dpr, low, high):
    masks = head_masks()
    ones = spread_heads(jnp.ones((128, 128), BF), masks)

    def attend(w, carry):
        sets = [slice(s * 128, (s + 1) * 128) for s in range(4)]
        t = []
        for s in range(4):
            v = spread_heads(pr[w, :, 1024 + s * 128 : 1024 + (s + 1) * 128], masks)
            g1 = ge[w, :, sets[s]]
            g2 = (-(g1.astype(F32) * mix[w, :, sets[s]].astype(F32))).astype(BF)
            t.append(dot(jnp.concatenate([g1, g2], 1), jnp.concatenate([v, ones], 1), NT))
        ds = [(es[w, s].astype(F32) * t[s]).astype(BF) for s in range(4)]
        dq, dk = [], []
        for s in range(4):
            k = spread_heads(pr[w, :, 512 + s * 128 : 512 + (s + 1) * 128], masks)
            dq.append(dot(ds[s], k) * SCALE)
            dk.append(merge_heads(dot(ds[s], pr[w, :, sets[s]], TN), masks) * SCALE)
        for s in range(4):
            dpr[w, :, sets[s]] = dq[s].astype(BF)
            dpr[w, :, 512 + s * 128 : 512 + (s + 1) * 128] = dk[s].astype(BF)
        return carry

    lax.fori_loop(low, high, attend, 0)


def backward_weights(n, dpr, put, kinds):
    for c in kinds:
        for j in range(2):
            cols = slice(c * 512 + j * 256, c * 512 + (j + 1) * 256)
            got = dot(n[...].reshape(512, 512), dpr[:, :, cols].reshape(512, 256), TN)
            put(c, j, got.astype(BF))


def backward_tokens(take, wq, cw, dpr, put, work, low, high):
    count = high - low
    grad = dot(dpr[low:high, :, 0:512].reshape(count * 128, 512), wq[0], NT)
    for c in (1, 2):
        part = dpr[low:high, :, c * 512 : (c + 1) * 512].reshape(count * 128, 512)
        grad = grad + dot(part, wq[c], NT)
    work[low:high] = grad.reshape(count, 128, 512)

    def finish(w, carry):
        grad = work[w]
        standard, inv = standardize(take(w).astype(F32))
        back = inv * (
            grad
            - jnp.mean(grad, -1, keepdims=True)
            - standard * jnp.mean(grad * standard, -1, keepdims=True)
        )
        put(w, cw[w].astype(F32) + back)
        return carry

    lax.fori_loop(low, high, finish, 0)


class Sum:
    def __init__(self, go, g, f, r0, a0, r1, a1, r2, a2, r3):
        self.go, self.g, self.f = go, g, f
        self.r0, self.a0, self.r1, self.a1, self.r2, self.a2, self.r3 = r0, a0, r1, a1, r2, a2, r3
        lat, lon, mp = place()
        self.mp, self.core, z = mp, lax.rem(lon, 2), lon // 2
        y, self.x_hi = lax.rem(lat, 4), lat // 4
        self.near = (lat, lon, 1 - mp)
        self.far = (lax.rem(lat + 4, 8), lon, 1 - mp)
        self.opposite = (lax.rem(lat + 4, 8), lon, mp)
        self.sibling = (lat, lon + 1 - 2 * self.core, mp)

        def along_y(step):
            return (lat // 4 * 4 + lax.rem(y + step, 4), lon, mp)

        def along_z(step):
            return (lat, lax.rem(z + step, 4) * 2 + lax.rem(lon, 2), mp)

        self.ways = ((y, along_y, z, along_z), (z, along_z, y, along_y))
        self.peers = [self.near, self.far, self.opposite, self.sibling]
        self.peers += [along_y(s) for s in (1, 2, 3)] + [along_z(s) for s in (1, 2, 3)]
        self.flying = []

    def wait(self):
        for copy in self.flying:
            copy.wait()
        self.flying = []

    def step0(self):
        self.flying = [self.go(self.g.at[:, 1 - self.core], self.r0, self.sibling)]

    def step1(self):
        self.wait()
        g, r0, a0, core = self.g, self.r0, self.a0, self.core

        def fold(n, carry):
            part, a = n // 4, lax.rem(n, 4)
            mine = g[:, core, part, a].astype(F32)
            a0[:, part, a] = (mine + r0[:, part, a].astype(F32)).astype(BF)
            return carry

        lax.fori_loop(0, 8, fold, 0)
        for step in (1, 2, 3):
            for part, (ia, along_a, ib, along_b) in enumerate(self.ways):
                to = lax.rem(ia + step, 4)
                self.flying.append(
                    self.go(a0.at[:, part, to], self.r1.at[part, step - 1], along_a(step))
                )

    def step2(self):
        self.wait()
        a0, r1, a1 = self.a0, self.r1, self.a1
        for part, (ia, along_a, ib, along_b) in enumerate(self.ways):

            def fold(b, carry):
                total = a0[:, part, ia, b].astype(F32)
                for k in range(3):
                    total = total + r1[part, k, :, b].astype(F32)
                a1[:, part, b] = total.astype(BF)
                return carry

            lax.fori_loop(0, 4, fold, 0)
        for step in (1, 2, 3):
            for part, (ia, along_a, ib, along_b) in enumerate(self.ways):
                to = lax.rem(ib + step, 4)
                self.flying.append(
                    self.go(a1.at[:, part, to], self.r2.at[part, step - 1], along_b(step))
                )

    def step3(self):
        self.wait()
        a1, r2, a2, r3, mp = self.a1, self.r2, self.a2, self.r3, self.mp
        for part, (ia, along_a, ib, along_b) in enumerate(self.ways):
            total = a1[:, part, ib].astype(F32)
            for k in range(3):
                total = total + r2[part, k].astype(F32)
            a2[:, part] = total.astype(BF)
        self.flying = [
            self.go(a2.at[1 - mp], r3.at[0], self.near),
            self.go(a2.at[1 - mp], r3.at[1], self.far),
            self.go(a2.at[mp], r3.at[2], self.opposite),
        ]

    def step4(self):
        self.wait()
        same = self.a2[self.mp].astype(F32) + self.r3[2].astype(F32)
        other = self.r3[0].astype(F32) + self.r3[1].astype(F32)
        total = (same + other).astype(BF)
        for part, (ia, along_a, ib, along_b) in enumerate(self.ways):
            self.f[self.core, part, ia, ib] = total[part]
        for step in (1, 2, 3):
            for part, (ia, along_a, ib, along_b) in enumerate(self.ways):
                spot = self.f.at[self.core, part, ia, ib]
                self.flying.append(self.go(spot, spot, along_b(step)))

    def step5(self):
        self.wait()
        self.coming = []
        for step in (1, 2, 3):
            for part, (ia, along_a, ib, along_b) in enumerate(self.ways):
                spot = self.f.at[self.core, part, ia]
                arrives = self.f.at[self.core, part, lax.rem(ia + 4 - step, 4)]
                self.coming.append((self.go(spot, spot, along_a(step)), arrives))
        for part, (ia, along_a, ib, along_b) in enumerate(self.ways):
            spot = self.f.at[self.core, part, ia]
            self.flying.append(self.go(spot, spot, self.sibling))

    def step6(self):
        for copy, spot in self.coming:
            copy.wait_recv()
            self.flying.append(self.go(spot, spot, self.sibling))

    def last(self):
        self.wait()
        for copy, _ in self.coming:
            copy.wait_send()


def around(lat, lon, mp, step):
    row_lat, row_mp = row_step(lat, mp, step)
    col = lax.rem(lon + step + 8, 8)
    return (row_lat, lon, row_mp), (lat, col, mp), (row_lat, col, row_mp)


SENDS = 176


def pair_kernel(
    fc, cc, wqp, wop, wqs, wos,
    ro, gfo, f_early, f_late, f_shift,
    x, hx, cx, rs, rp, gs, gp, gf, rn,
    fqp, fop, fqs, fos,
    n_p, pr_p, es_p, rd_p, mix_p,
    n_s, pr_s, es_s, rd_s, mix_s,
    cw, do, dpr, ge, cn,
    g_early, g_late, g_shift,
    *rest,
):
    sums, (send, recv, local) = rest[:21], rest[21:]
    lat, lon, mp = place()
    row_prev, col_prev, corner_prev = around(lat, lon, mp, -1)
    row_next, col_next, corner_next = around(lat, lon, mp, 1)
    go = Sender(send, recv)
    early = Sum(go, g_early, f_early, *sums[:7])
    late = Sum(go, g_late, f_late, *sums[7:14])
    shifted = Sum(go, g_shift, f_shift, *sums[14:])
    near, far, sibling, core = early.near, early.far, early.sibling, early.core
    barrier(
        early.peers
        + [row_prev, col_prev, corner_prev, row_next, col_next, corner_next]
    )
    lanes = pl.ds(pl.multiple_of(mp * 256, 256), 256)
    away = pl.ds(pl.multiple_of((1 - mp) * 256, 256), 256)
    other_rows = pl.ds((1 - mp) * 16, 16)
    own_rows = pl.ds(mp * 16, 16)
    own = pl.ds(0, 4)
    kept = []

    def keep(src, dst):
        copy = pltpu.make_async_copy(src, dst, local.at[len(kept)])
        copy.start()
        kept.append(copy)
        return copy

    def weight(src, dst, c, peer):
        rows = pl.ds(pl.multiple_of(core * 256, 256), 256)
        return go(src.at[c, rows], dst.at[c, rows, lanes], peer), dst.at[c, rows, away]

    def weight_out(src, dst, peer):
        rows = pl.ds(pl.multiple_of(core * 128, 128), 128)
        there = pl.ds(pl.multiple_of(mp * 256 + core * 128, 128), 128)
        here = pl.ds(pl.multiple_of((1 - mp) * 256 + core * 128, 128), 128)
        return go(src.at[rows], dst.at[there], peer), dst.at[here]

    y, z = lax.rem(lat, 4), lon // 2
    along_y, along_z = early.ways[0][1], early.ways[0][3]
    rows_s = pl.ds(pl.multiple_of(core * 256 + y * 64, 64), 64)
    half_s = pl.ds(pl.multiple_of(core * 256, 256), 256)
    at_o = core * 128 + z * 32
    rows_o = pl.ds(pl.multiple_of(at_o, 32), 32)
    there_o = pl.ds(pl.multiple_of(mp * 256 + at_o, 32), 32)
    here_o = pl.ds(pl.multiple_of((1 - mp) * 256 + at_o, 32), 32)
    half_o = pl.ds(pl.multiple_of((1 - mp) * 256 + core * 128, 128), 128)

    unsent = []

    def pass_on(part):
        copy, spot = part
        copy.wait_recv()
        unsent.append(copy)
        passed = go(spot, spot, sibling)
        unsent.append(passed)
        return passed

    fields_copy = go(fc.at[other_rows], x.at[:, :, lanes], near)
    qkv_p = [weight(wqp, fqp, c, far) for c in range(3)]
    x_kept = keep(fc.at[own_rows], x.at[:, :, lanes])
    mp_rows = pl.ds(pl.multiple_of(mp * 256, 256), 256)
    others = [
        keep(wqp, fqp.at[:, :, lanes]),
        keep(wop, fop.at[mp_rows]),
        keep(wqs, fqs.at[:, :, lanes]),
        keep(wos, fos.at[mp_rows]),
        keep(cc.at[own_rows], cn.at[:, :, lanes]),
    ]

    def take_x(w):
        return rows_window(x, w)

    def put_hidden(w, value):
        put_window(hx, w, cells_of(value).astype(BF))

    fields_copy.wait()
    x_kept.wait()
    over_x = [
        go(wqs.at[:, rows_s], fqs.at[:, rows_s, lanes], near),
        go(wos.at[rows_o], fos.at[there_o], near),
    ]
    forward_norm(take_x, n_p, 0, 4)
    for copy in others:
        copy.wait()
    forward_project(n_p, fqp, pr_p, 0, 4, (mp,))
    passed = [pass_on(part) for part in qkv_p]
    out_p = weight_out(wop, fop, far)
    forward_attend(pr_p, es_p, rd_p, mix_p, None, 0, 4, (mp * 2, mp * 2 + 1))
    for copy in passed:
        copy.wait_recv()
    forward_project(n_p, fqp, pr_p, 0, 4, (1 - mp,))
    for copy in over_x:
        copy.wait_recv()
    unsent.extend(over_x)
    spread = []
    for step in (1, 2, 3):
        spot = fqs.at[:, rows_s, away]
        spread.append(go(spot, spot, along_y(step)))
        spot = fos.at[here_o]
        spread.append(go(spot, spot, along_z(step)))
    cot_copy = go(cc.at[other_rows], cn.at[:, :, lanes], near)
    others_sets = (2 - mp * 2, 3 - mp * 2)
    forward_attend(pr_p, es_p, rd_p, mix_p, None, 0, 3, others_sets)
    pass_on(out_p).wait_recv()
    forward_out(take_x, fop, mix_p, put_hidden, do, 0, 3)

    halos = [
        go(hx.at[0, own], hx.at[4, own], row_prev),
        go(hx.at[own, 0], hx.at[own, 4], col_prev),
        go(hx.at[0, 0], hx.at[4, 4], corner_prev),
    ]
    forward_attend(pr_p, es_p, rd_p, mix_p, None, 3, 4, others_sets)
    forward_out(take_x, fop, mix_p, put_hidden, do, 3, 4)

    def take_hidden(w):
        return window(hx, w, 1)

    for copy in spread:
        copy.wait()
    spot = fqs.at[:, half_s, away]
    passed_qkv = go(spot, spot, sibling)
    spot = fos.at[half_o]
    passed_out = go(spot, spot, sibling)
    forward_norm(take_hidden, n_s, 0, 1)
    passed_qkv.wait()
    forward_project(n_s, fqs, pr_s, 0, 1)
    cut = (lat * 2 + mp) == 15
    forward_attend(pr_s, es_s, rd_s, mix_s, cut, 0, 1)

    cot_copy.wait()

    def into_cells(w, carry):
        put_window(cx, w, cells_of(rows_window(cn, w).astype(F32)).astype(BF))
        return carry

    lax.fori_loop(0, 4, into_cells, 0)
    for copy in halos:
        copy.wait()
    cot_halos = [
        go(cx.at[0, own], cx.at[4, own], row_prev),
        go(cx.at[own, 0], cx.at[own, 4], col_prev),
        go(cx.at[0, 0], cx.at[4, 4], corner_prev),
    ]
    forward_norm(take_hidden, n_s, 1, 4)
    forward_project(n_s, fqs, pr_s, 1, 4)
    forward_attend(pr_s, es_s, rd_s, mix_s, cut, 1, 4)
    passed_out.wait()

    def put_result(w, value):
        put_window(rs, w, value.astype(BF))

    forward_out(take_hidden, fos, mix_s, put_result, do, 0, 4)

    low, high = pl.ds(0, 3), pl.ds(1, 3)

    def narrow(src, dst):
        return [
            go(src.at[3, low], dst.at[0, high], row_next),
            go(src.at[low, 3], dst.at[high, 0], col_next),
            go(src.at[3, 3], dst.at[0, 0], corner_next),
        ]

    result_halos = narrow(rs, rp)
    result_halos.append(keep(rs.at[low, low], rp.at[high, high]))

    def take_cot(w):
        return window(cx, w, 1)

    def put_grad(w, value):
        put_window(gs, w, value.astype(BF))

    def put_shift(kind, j, value):
        g_shift[j, kind // 2, kind % 2] = value.reshape(4, 4, 2, 16, 256)

    for copy in cot_halos:
        copy.wait()
    for first, end in ((1, 4), (0, 1)):
        backward_do(take_cot, fos, cw, do, first, end)
        backward_values(es_s, rd_s, do, ge, dpr, first, end)
        backward_scores(pr_s, es_s, mix_s, ge, dpr, first, end)
        backward_tokens(take_hidden, fqs, cw, dpr, put_grad, do, first, end)
        if first == 1:
            grad_halos = narrow(gs, gp)
    grad_kept = keep(gs.at[low, low], gp.at[high, high])
    backward_out(mix_s, cw, put_shift)
    backward_weights(n_s, dpr, put_shift, (0, 1, 2))
    shifted.step0()
    for copy in result_halos:
        copy.wait()

    def into_rows(w, carry):
        put_rows(rn, w, rows_of(window(rp, w, 0).astype(F32)).astype(BF))
        return carry

    lax.fori_loop(0, 4, into_rows, 0)
    ends = [go(rn.at[:, :, away], ro.at[own_rows], near)]
    ends.append(keep(rn.at[:, :, lanes], ro.at[own_rows]))

    def take_back(w):
        return rows_of(window(gp, w, 0).astype(F32)).astype(BF)

    def put_fields(w, value):
        put_rows(gf, w, value.astype(BF))

    def put_plain(kind, j, value):
        to = g_early if kind >= 2 else g_late
        for part in range(2):
            half = value[:, part * 128 : (part + 1) * 128]
            to[j, kind % 2, part] = half.reshape(4, 4, 2, 16, 128)

    grad_kept.wait()
    backward_do(take_back, fop, cw, do, 3, 4)
    backward_values(es_p, rd_p, do, ge, dpr, 3, 4)
    backward_scores(pr_p, es_p, mix_p, ge, dpr, 3, 4)
    for copy in grad_halos:
        copy.wait()
    shifted.step1()
    backward_do(take_back, fop, cw, do, 0, 3)
    backward_values(es_p, rd_p, do, ge, dpr, 0, 3)
    backward_weights(n_p, dpr, put_plain, (2,))
    backward_out(mix_p, cw, put_plain)
    early.step0()
    backward_scores(pr_p, es_p, mix_p, ge, dpr, 0, 3)
    early.step1()
    backward_weights(n_p, dpr, put_plain, (0, 1))
    late.step0()
    for half in range(2):
        backward_tokens(take_x, fqp, cw, dpr, put_fields, do, half * 2, half * 2 + 2)
        rows = pl.ds(half * 8, 8)
        there = pl.ds(mp * 16 + half * 8, 8)
        ends.append(go(gf.at[rows, :, away], gfo.at[there], near))
        ends.append(keep(gf.at[rows, :, lanes], gfo.at[there]))
        if half == 0:
            late.step1()
            shifted.step2()
    early.step2()
    shifted.step3()
    late.step2()
    early.step3()
    shifted.step4()
    late.step3()
    early.step4()
    shifted.step5()
    late.step4()
    early.step5()
    shifted.step6()
    late.step5()
    early.step6()
    late.step6()
    shifted.last()
    early.last()
    late.last()
    for copy in ends:
        copy.wait()
    for copy in unsent:
        copy.wait_send()


def last_kernel(
    factor, f_early, f_late, f_shift, r, gf,
    qkv_p, out_p, qkv_s, out_s, ro, gfo,
    raw, wide, held, came, gone,
):
    coming, going = [], []

    def move(src, dst, sem, to):
        copy = pltpu.make_async_copy(src, dst, sem)
        copy.start()
        to.append(copy)

    for n in range(4):
        move(f_shift.at[pl.ds(n * 512, 512)], raw.at[n], came.at[n], coming)
    for n, src in enumerate((r, gf)):
        move(src, held.at[n], came.at[4 + n], coming)
    for n in range(4):
        for part in range(2):
            src = (f_late, f_early)[n // 2].at[n % 2, part]
            dst = raw.at[4 + n, :, pl.ds(part * 128, 128)]
            move(src, dst, came.at[6 + n * 2 + part], coming)
    for n in range(8):
        if n < 4:
            coming[n].wait()
        else:
            coming[n * 2 - 2].wait()
            coming[n * 2 - 1].wait()
        wide[n] = raw[n].astype(F32) * factor
        if n % 4 < 3:
            move(wide.at[n], (qkv_s, qkv_p)[n // 4].at[n % 4], gone.at[n], going)
        else:
            for k in range(2):
                cols = pl.ds(k * 256, 256)
                dst = (out_s, out_p)[n // 4].at[:, cols]
                move(wide.at[n, cols], dst, gone.at[8 + n // 4 * 2 + k], going)
    for n, dst in enumerate((ro, gfo)):
        coming[4 + n].wait()
        move(held.at[n], dst, gone.at[12 + n], going)
    for copy in going:
        copy.wait()


def shape(*dims, dtype=BF):
    return jax.ShapeDtypeStruct(dims, dtype)


GRID = (4, 4, 32, 512)
WIDE = (5, 5, 32, 512)
ROWS = (16, 32, 512)
HELD = (32, 32, 256)
SAVED = (
    ((4, 128, 512), BF),
    ((4, 128, 1536), BF),
    ((4, 4, 128, 512), BF),
    ((4, 128, 512), F32),
    ((4, 128, 512), BF),
)


def sum_shapes(width):
    return [
        (2, 2, 4, 4, 2, 16, width),
        (2, 2, 4, 4, 2, 16, width),
        (2, 3, 2, 4, 2, 16, width),
        (2, 2, 4, 2, 16, width),
        (2, 3, 2, 2, 16, width),
        (2, 2, 2, 16, width),
        (3, 2, 2, 16, width),
    ]


SCRATCH = (
    [(s, BF) for s in (ROWS, WIDE, WIDE, GRID, GRID, GRID, GRID, ROWS, ROWS)]
    + [((3, 512, 512), BF), ((512, 512), BF)] * 2
    + list(SAVED) * 2
    + [((4, 128, 512), BF), ((4, 128, 512), F32), ((4, 128, 1536), BF), ((4, 128, 512), BF), (ROWS, BF)]
    + [((2, 2, 2, 4, 4, 2, 16, width), BF) for width in (128, 128, 256)]
    + [(s, BF) for width in (128, 128, 256) for s in sum_shapes(width)]
)


def on_device(fields, qkv_plain, out_plain, qkv_shift, out_shift, cotangent):
    factor = (fields.shape[0] * fields.shape[1] * 64) ** -0.5
    vmem = pl.BlockSpec(memory_space=pltpu.VMEM)
    hbm = pl.BlockSpec(memory_space=pl.ANY)
    f_half, f_whole = (2, 2, 4, 4, 2, 16, 128), (2, 2, 4, 4, 2, 16, 256)
    result, grad_fields, f_early, f_late, f_shift = pl.pallas_call(
        pair_kernel,
        out_shape=[shape(*HELD), shape(*HELD), shape(*f_half), shape(*f_half), shape(*f_whole)],
        in_specs=[hbm] * 6,
        out_specs=[vmem] * 5,
        scratch_shapes=[pltpu.VMEM(s, t) for s, t in SCRATCH]
        + [
            pltpu.SemaphoreType.DMA((SENDS,)),
            pltpu.SemaphoreType.DMA((SENDS,)),
            pltpu.SemaphoreType.DMA((12,)),
        ],
        compiler_params=pltpu.CompilerParams(
            collective_id=0, has_side_effects=True, vmem_limit_bytes=VMEM_LIMIT
        ),
    )(
        fields,
        cotangent,
        qkv_plain.transpose(1, 0, 2),
        out_plain,
        qkv_shift.transpose(1, 0, 2),
        out_shift,
    )
    qkv, out = shape(3, 512, 256, dtype=F32), shape(256, 512, dtype=F32)
    qkv_p, out_p, qkv_s, out_s, result, grad_fields = pl.pallas_call(
        functools.partial(last_kernel, factor),
        out_shape=[qkv, out, qkv, out, shape(*HELD), shape(*HELD)],
        in_specs=[hbm] * 5,
        out_specs=[hbm] * 6,
        scratch_shapes=[
            pltpu.VMEM((8, 512, 256), BF),
            pltpu.VMEM((8, 512, 256), F32),
            pltpu.VMEM((2,) + HELD, BF),
            pltpu.SemaphoreType.DMA((14,)),
            pltpu.SemaphoreType.DMA((14,)),
        ],
        compiler_params=pltpu.CompilerParams(vmem_limit_bytes=VMEM_LIMIT),
    )(
        f_early.reshape(2, 2, 512, 128),
        f_late.reshape(2, 2, 512, 128),
        f_shift.reshape(2048, 256),
        result,
        grad_fields,
    )
    return (
        result,
        grad_fields,
        qkv_p.transpose(1, 0, 2),
        out_p,
        qkv_s.transpose(1, 0, 2),
        out_s,
    )


def solution(mesh):
    in_specs = (
        P("lat", "lon", "mp"),
        P(None, None, "mp"),
        P("mp", None),
        P(None, None, "mp"),
        P("mp", None),
        P("lat", "lon", "mp"),
    )
    out_specs = (
        P("lat", "lon", "mp"),
        P("lat", "lon", "mp"),
        P(None, None, "mp"),
        P("mp", None),
        P(None, None, "mp"),
        P("mp", None),
    )
    return jax.shard_map(
        on_device, mesh=mesh, in_specs=in_specs, out_specs=out_specs, check_vma=False
    )
```

```python
import functools

import jax
import jax.numpy as jnp
from jax import lax
from jax.experimental import pallas as pl
from jax.experimental.pallas import tpu as pltpu
from jax.sharding import PartitionSpec as P

BF = jnp.bfloat16
F32 = jnp.float32
MESH = pl.DeviceIdType.MESH
VMEM_LIMIT = 56 * 1024 * 1024
D = 512
HEAD_DIM = 32
SCALE = HEAD_DIM ** -0.5
LOG2E = 1.4426950408889634


def place():
    lat, lon, mp = lax.axis_index("lat"), lax.axis_index("lon"), lax.axis_index("mp")
    return lat, lon, mp


def row_step(lat, mp, step):
    at = lax.rem(lat * 2 + mp + step + 16, 16)
    return at // 2, lax.rem(at, 2)


def barrier(peers):
    sem = pltpu.get_barrier_semaphore()
    for peer in peers:
        pl.semaphore_signal(sem, inc=1, device_id=peer, device_id_type=MESH)
    pl.semaphore_wait(sem, len(peers))


class Sender:
    def __init__(self, send, recv):
        self.send, self.recv, self.used = send, recv, 0

    def __call__(self, src, dst, peer):
        copy = pltpu.make_async_remote_copy(
            src_ref=src,
            dst_ref=dst,
            send_sem=self.send.at[self.used],
            recv_sem=self.recv.at[self.used],
            device_id=peer,
            device_id_type=MESH,
        )
        self.used += 1
        copy.start()
        return copy


NN = (((1,), (0,)), ((), ()))
NT = (((1,), (1,)), ((), ()))
TN = (((0,), (0,)), ((), ()))


def dot(left, right, dims=NN):
    return lax.dot_general(left, right, dims, preferred_element_type=F32)


def head_masks():
    lane = lax.broadcasted_iota(jnp.int32, (128, 128), 1) // HEAD_DIM
    return [lane == h for h in range(4)]


def spread_heads(block, masks):
    zero = jnp.zeros_like(block)
    return jnp.concatenate([jnp.where(m, block, zero) for m in masks], 0)


def merge_heads(tall, masks):
    total = jnp.where(masks[0], tall[0:128], 0.0)
    for h in range(1, 4):
        total = jnp.where(masks[h], tall[h * 128 : (h + 1) * 128], total)
    return total


def standardize(x):
    centred = x - jnp.mean(x, -1, keepdims=True)
    inv = lax.rsqrt(jnp.mean(centred * centred, -1, keepdims=True) + 1e-05)
    return centred * inv, inv


def window(ref, w, offset):
    i, j = w // 2, lax.rem(w, 2)
    got = ref[pl.ds(2 * i + offset, 2), pl.ds(2 * j + offset, 2)]
    return got.reshape(128, D)


def put_window(ref, w, value):
    i, j = w // 2, lax.rem(w, 2)
    ref[pl.ds(2 * i, 2), pl.ds(2 * j, 2)] = value.reshape(2, 2, 32, D)


def rows_window(ref, w):
    i, j = w // 2, lax.rem(w, 2)
    got = ref[pl.ds(8 * i, 8), pl.ds(pl.multiple_of(16 * j, 16), 16)]
    return got.reshape(128, D)


def put_rows(ref, w, value):
    i, j = w // 2, lax.rem(w, 2)
    ref[pl.ds(8 * i, 8), pl.ds(pl.multiple_of(16 * j, 16), 16)] = value.reshape(8, 16, D)


def cells_of(value):
    return value.reshape(2, 4, 2, 8, D).transpose(0, 2, 1, 3, 4).reshape(128, D)


def rows_of(value):
    return value.reshape(2, 2, 4, 8, D).transpose(0, 2, 1, 3, 4).reshape(128, D)


def forward_norm(take, n, low, high):
    def norm(w, carry):
        n[w] = standardize(take(w).astype(F32))[0].astype(BF)
        return carry

    lax.fori_loop(low, high, norm, 0)


def lanes_at(start, size):
    if isinstance(start, int):
        return slice(start, start + size)
    return pl.ds(pl.multiple_of(start, size), size)


def forward_project(n, wq, pr, low, high, groups=(0, 1)):
    count = high - low
    for j in groups:
        for c in range(3):
            weight = wq[c, :, lanes_at(j * 256, 256)]
            got = dot(n[low:high].reshape(count * 128, 512), weight)
            pr[low:high, :, lanes_at(c * 512 + j * 256, 256)] = got.astype(BF).reshape(count, 128, 256)


def forward_attend(pr, es, rd, mix, cut, low, high, chosen=(0, 1, 2, 3)):
    masks = head_masks()
    ones = spread_heads(jnp.ones((128, 128), BF), masks)
    if cut is not None:
        q_half = lax.broadcasted_iota(jnp.int32, (128, 512), 0) // 64
        k_half = lax.rem(lax.broadcasted_iota(jnp.int32, (128, 512), 1) // 64, 2)
        same = q_half == k_half

    def attend(w, carry):
        scores = []
        for s in chosen:
            q = pr[w, :, lanes_at(s * 128, 128)]
            k = spread_heads(pr[w, :, lanes_at(512 + s * 128, 128)], masks)
            scores.append(dot(q, k, NT))
        es_now = []
        for score in scores:
            e = jnp.exp2(score * (SCALE * LOG2E))
            if cut is not None:
                e = jnp.where(same | jnp.logical_not(cut & (w >= 2)), e, 0.0)
            es_now.append(e.astype(BF))
        both = []
        for s, e in zip(chosen, es_now):
            v = spread_heads(pr[w, :, lanes_at(1024 + s * 128, 128)], masks)
            both.append(dot(e, jnp.concatenate([v, ones], 1)))
        for s, e, pair in zip(chosen, es_now, both):
            es[w, s] = e
            inv = 1.0 / pair[:, 128:]
            rd[w, :, lanes_at(s * 128, 128)] = inv
            mix[w, :, lanes_at(s * 128, 128)] = (pair[:, :128] * inv).astype(BF)
        return carry

    lax.fori_loop(low, high, attend, 0, unroll=2 if (high - low) % 2 == 0 else 1)


def forward_out(take, wo, mix, put, work, low, high):
    count = high - low
    got = dot(mix[low:high].reshape(count * 128, 512), wo[...])
    work[low:high] = got.reshape(count, 128, 512)

    def project(w, carry):
        put(w, take(w).astype(F32) + work[w])
        return carry

    lax.fori_loop(low, high, project, 0)


def backward_do(take, wo, cw, do, low, high):
    count = high - low

    def gather(w, carry):
        cw[w] = take(w)
        return carry

    lax.fori_loop(low, high, gather, 0)
    for j in range(2):
        cols = slice(j * 256, (j + 1) * 256)
        got = dot(cw[low:high].reshape(count * 128, 512), wo[cols, :], NT)
        do[low:high, :, cols] = got.reshape(count, 128, 256)


def backward_out(mix, cw, put):
    for j in range(2):
        cols = slice(j * 256, (j + 1) * 256)
        got = dot(mix[:, :, cols].reshape(512, 256), cw[...].reshape(512, 512), TN).astype(BF)
        put(3, j, jnp.concatenate([got[:, 0:256], got[:, 256:512]], 0))


def backward_values(es, rd, do, ge, dpr, low, high):
    masks = head_masks()

    def attend(w, carry):
        sets = [slice(s * 128, (s + 1) * 128) for s in range(4)]
        g1 = [(do[w, :, lanes] * rd[w, :, lanes]).astype(BF) for lanes in sets]
        tall = [dot(es[w, s], g1[s], TN) for s in range(4)]
        for s in range(4):
            ge[w, :, sets[s]] = g1[s]
            dv = merge_heads(tall[s], masks)
            dpr[w, :, 1024 + s * 128 : 1024 + (s + 1) * 128] = dv.astype(BF)
        return carry

    lax.fori_loop(low, high, attend, 0, unroll=2 if (high - low) % 2 == 0 else 1)


def backward_scores(pr, es, mix, ge, dpr, low, high):
    masks = head_masks()
    ones = spread_heads(jnp.ones((128, 128), BF), masks)

    def attend(w, carry):
        sets = [slice(s * 128, (s + 1) * 128) for s in range(4)]
        t = []
        for s in range(4):
            v = spread_heads(pr[w, :, 1024 + s * 128 : 1024 + (s + 1) * 128], masks)
            g1 = ge[w, :, sets[s]]
            g2 = (-(g1.astype(F32) * mix[w, :, sets[s]].astype(F32))).astype(BF)
            t.append(dot(jnp.concatenate([g1, g2], 1), jnp.concatenate([v, ones], 1), NT))
        ds = [(es[w, s].astype(F32) * t[s]).astype(BF) for s in range(4)]
        dq, dk = [], []
        for s in range(4):
            k = spread_heads(pr[w, :, 512 + s * 128 : 512 + (s + 1) * 128], masks)
            dq.append(dot(ds[s], k) * SCALE)
            dk.append(merge_heads(dot(ds[s], pr[w, :, sets[s]], TN), masks) * SCALE)
        for s in range(4):
            dpr[w, :, sets[s]] = dq[s].astype(BF)
            dpr[w, :, 512 + s * 128 : 512 + (s + 1) * 128] = dk[s].astype(BF)
        return carry

    lax.fori_loop(low, high, attend, 0, unroll=2 if (high - low) % 2 == 0 else 1)


def backward_weights(n, dpr, put, kinds):
    for c in kinds:
        for j in range(2):
            cols = slice(c * 512 + j * 256, c * 512 + (j + 1) * 256)
            got = dot(n[...].reshape(512, 512), dpr[:, :, cols].reshape(512, 256), TN)
            put(c, j, got.astype(BF))


def backward_tokens(take, wq, cw, dpr, put, work, low, high):
    count = high - low
    grad = dot(dpr[low:high, :, 0:512].reshape(count * 128, 512), wq[0], NT)
    for c in (1, 2):
        part = dpr[low:high, :, c * 512 : (c + 1) * 512].reshape(count * 128, 512)
        grad = grad + dot(part, wq[c], NT)
    work[low:high] = grad.reshape(count, 128, 512)

    def finish(w, carry):
        grad = work[w]
        standard, inv = standardize(take(w).astype(F32))
        back = inv * (
            grad
            - jnp.mean(grad, -1, keepdims=True)
            - standard * jnp.mean(grad * standard, -1, keepdims=True)
        )
        put(w, cw[w].astype(F32) + back)
        return carry

    lax.fori_loop(low, high, finish, 0)


class Sum:
    def __init__(self, go, g, f, r0, a0, r1, a1, r2, a2, r3):
        self.go, self.g, self.f = go, g, f
        self.r0, self.a0, self.r1, self.a1, self.r2, self.a2, self.r3 = r0, a0, r1, a1, r2, a2, r3
        lat, lon, mp = place()
        self.mp, self.core, z = mp, lax.rem(lon, 2), lon // 2
        y, self.x_hi = lax.rem(lat, 4), lat // 4
        self.near = (lat, lon, 1 - mp)
        self.far = (lax.rem(lat + 4, 8), lon, 1 - mp)
        self.opposite = (lax.rem(lat + 4, 8), lon, mp)
        self.sibling = (lat, lon + 1 - 2 * self.core, mp)

        def along_y(step):
            return (lat // 4 * 4 + lax.rem(y + step, 4), lon, mp)

        def along_z(step):
            return (lat, lax.rem(z + step, 4) * 2 + lax.rem(lon, 2), mp)

        self.ways = ((y, along_y, z, along_z), (z, along_z, y, along_y))
        self.peers = [self.near, self.far, self.opposite, self.sibling]
        self.peers += [along_y(s) for s in (1, 2, 3)] + [along_z(s) for s in (1, 2, 3)]
        self.flying = []

    def wait(self):
        for copy in self.flying:
            copy.wait()
        self.flying = []

    def step0(self):
        self.flying = [self.go(self.g.at[:, 1 - self.core], self.r0, self.sibling)]

    def step1(self):
        self.wait()
        g, r0, a0, core = self.g, self.r0, self.a0, self.core

        def fold(n, carry):
            part, a = n // 4, lax.rem(n, 4)
            mine = g[:, core, part, a].astype(F32)
            a0[:, part, a] = (mine + r0[:, part, a].astype(F32)).astype(BF)
            return carry

        lax.fori_loop(0, 8, fold, 0)
        for step in (1, 2, 3):
            for part, (ia, along_a, ib, along_b) in enumerate(self.ways):
                to = lax.rem(ia + step, 4)
                self.flying.append(
                    self.go(a0.at[:, part, to], self.r1.at[part, step - 1], along_a(step))
                )

    def step2(self):
        self.wait()
        a0, r1, a1 = self.a0, self.r1, self.a1
        for part, (ia, along_a, ib, along_b) in enumerate(self.ways):

            def fold(b, carry):
                total = a0[:, part, ia, b].astype(F32)
                for k in range(3):
                    total = total + r1[part, k, :, b].astype(F32)
                a1[:, part, b] = total.astype(BF)
                return carry

            lax.fori_loop(0, 4, fold, 0)
        for step in (1, 2, 3):
            for part, (ia, along_a, ib, along_b) in enumerate(self.ways):
                to = lax.rem(ib + step, 4)
                self.flying.append(
                    self.go(a1.at[:, part, to], self.r2.at[part, step - 1], along_b(step))
                )

    def step3(self):
        self.wait()
        a1, r2, a2, r3, mp = self.a1, self.r2, self.a2, self.r3, self.mp
        for part, (ia, along_a, ib, along_b) in enumerate(self.ways):
            total = a1[:, part, ib].astype(F32)
            for k in range(3):
                total = total + r2[part, k].astype(F32)
            a2[:, part] = total.astype(BF)
        self.flying = [
            self.go(a2.at[1 - mp], r3.at[0], self.near),
            self.go(a2.at[1 - mp], r3.at[1], self.far),
            self.go(a2.at[mp], r3.at[2], self.opposite),
        ]

    def step4(self):
        self.wait()
        same = self.a2[self.mp].astype(F32) + self.r3[2].astype(F32)
        other = self.r3[0].astype(F32) + self.r3[1].astype(F32)
        total = (same + other).astype(BF)
        for part, (ia, along_a, ib, along_b) in enumerate(self.ways):
            self.f[self.core, part, ia, ib] = total[part]
        for step in (1, 2, 3):
            for part, (ia, along_a, ib, along_b) in enumerate(self.ways):
                spot = self.f.at[self.core, part, ia, ib]
                self.flying.append(self.go(spot, spot, along_b(step)))

    def step5(self):
        self.wait()
        self.coming = []
        for step in (1, 2, 3):
            for part, (ia, along_a, ib, along_b) in enumerate(self.ways):
                spot = self.f.at[self.core, part, ia]
                arrives = self.f.at[self.core, part, lax.rem(ia + 4 - step, 4)]
                self.coming.append((self.go(spot, spot, along_a(step)), arrives))
        for part, (ia, along_a, ib, along_b) in enumerate(self.ways):
            spot = self.f.at[self.core, part, ia]
            self.flying.append(self.go(spot, spot, self.sibling))

    def step6(self):
        for copy, spot in self.coming:
            copy.wait_recv()
            self.flying.append(self.go(spot, spot, self.sibling))

    def last(self):
        self.wait()
        for copy, _ in self.coming:
            copy.wait_send()


def around(lat, lon, mp, step):
    row_lat, row_mp = row_step(lat, mp, step)
    col = lax.rem(lon + step + 8, 8)
    return (row_lat, lon, row_mp), (lat, col, mp), (row_lat, col, row_mp)


SENDS = 176


def pair_kernel(
    fc, cc, wqp, wop, wqs, wos,
    ro, gfo, f_early, f_late, f_shift,
    x, hx, cx, rs, rp, gs, gp, gf, rn,
    fqp, fop, fqs, fos,
    n_p, pr_p, es_p, rd_p, mix_p,
    n_s, pr_s, es_s, rd_s, mix_s,
    cw, do, dpr, ge, cn,
    g_early, g_late, g_shift,
    *rest,
):
    sums, (send, recv, local) = rest[:21], rest[21:]
    lat, lon, mp = place()
    row_prev, col_prev, corner_prev = around(lat, lon, mp, -1)
    row_next, col_next, corner_next = around(lat, lon, mp, 1)
    go = Sender(send, recv)
    early = Sum(go, g_early, f_early, *sums[:7])
    late = Sum(go, g_late, f_late, *sums[7:14])
    shifted = Sum(go, g_shift, f_shift, *sums[14:])
    near, far, sibling, core = early.near, early.far, early.sibling, early.core
    barrier(
        early.peers
        + [row_prev, col_prev, corner_prev, row_next, col_next, corner_next]
    )
    lanes = pl.ds(pl.multiple_of(mp * 256, 256), 256)
    away = pl.ds(pl.multiple_of((1 - mp) * 256, 256), 256)
    other_rows = pl.ds((1 - mp) * 16, 16)
    other_half = [pl.ds((1 - mp) * 16 + half * 8, 8) for half in range(2)]
    own_rows = pl.ds(mp * 16, 16)
    own = pl.ds(0, 4)
    kept = []

    def keep(src, dst):
        copy = pltpu.make_async_copy(src, dst, local.at[len(kept)])
        copy.start()
        kept.append(copy)
        return copy

    def weight(src, dst, c, peer):
        rows = pl.ds(pl.multiple_of(core * 256, 256), 256)
        return go(src.at[c, rows], dst.at[c, rows, lanes], peer), dst.at[c, rows, away]

    def weight_out(src, dst, peer):
        rows = pl.ds(pl.multiple_of(core * 128, 128), 128)
        there = pl.ds(pl.multiple_of(mp * 256 + core * 128, 128), 128)
        here = pl.ds(pl.multiple_of((1 - mp) * 256 + core * 128, 128), 128)
        return go(src.at[rows], dst.at[there], peer), dst.at[here]

    y, z = lax.rem(lat, 4), lon // 2
    along_y, along_z = early.ways[0][1], early.ways[0][3]
    rows_s = pl.ds(pl.multiple_of(core * 256 + y * 64, 64), 64)
    half_s = pl.ds(pl.multiple_of(core * 256, 256), 256)
    at_o = core * 128 + z * 32
    rows_o = pl.ds(pl.multiple_of(at_o, 32), 32)
    there_o = pl.ds(pl.multiple_of(mp * 256 + at_o, 32), 32)
    here_o = pl.ds(pl.multiple_of((1 - mp) * 256 + at_o, 32), 32)
    half_o = pl.ds(pl.multiple_of((1 - mp) * 256 + core * 128, 128), 128)

    unsent = []

    def pass_on(part):
        copy, spot = part
        copy.wait_recv()
        unsent.append(copy)
        passed = go(spot, spot, sibling)
        unsent.append(passed)
        return passed

    fields_copy = [
        go(fc.at[other_half[half]], x.at[pl.ds(half * 8, 8), :, lanes], near) for half in range(2)
    ]
    qkv_p = [weight(wqp, fqp, c, far) for c in range(3)]
    out_p = weight_out(wop, fop, far)
    over_x = [
        go(wqs.at[:, rows_s], fqs.at[:, rows_s, lanes], near),
        go(wos.at[rows_o], fos.at[there_o], near),
    ]
    cot_copy = go(cc.at[other_rows], cn.at[:, :, lanes], near)
    x_kept = keep(fc.at[own_rows], x.at[:, :, lanes])
    mp_rows = pl.ds(pl.multiple_of(mp * 256, 256), 256)
    others = [
        keep(wqp, fqp.at[:, :, lanes]),
        keep(wop, fop.at[mp_rows]),
        keep(wqs, fqs.at[:, :, lanes]),
        keep(wos, fos.at[mp_rows]),
        keep(cc.at[own_rows], cn.at[:, :, lanes]),
    ]

    def take_x(w):
        return rows_window(x, w)

    def put_hidden(w, value):
        put_window(hx, w, cells_of(value).astype(BF))

    x_kept.wait()
    for half in range(2):
        fields_copy[half].wait()
        forward_norm(take_x, n_p, half * 2, half * 2 + 2)
        if half == 0:
            for copy in others:
                copy.wait()
        forward_project(n_p, fqp, pr_p, half * 2, half * 2 + 2, (mp,))
    passed = [pass_on(part) for part in qkv_p]
    for copy in over_x:
        copy.wait_recv()
    unsent.extend(over_x)
    spread = []
    for step in (1, 2, 3):
        spot = fqs.at[:, rows_s, away]
        spread.append(go(spot, spot, along_y(step)))
        spot = fos.at[here_o]
        spread.append(go(spot, spot, along_z(step)))
    forward_attend(pr_p, es_p, rd_p, mix_p, None, 0, 4, (mp * 2, mp * 2 + 1))
    for copy in passed:
        copy.wait_recv()
    forward_project(n_p, fqp, pr_p, 0, 4, (1 - mp,))
    others_sets = (2 - mp * 2, 3 - mp * 2)
    forward_attend(pr_p, es_p, rd_p, mix_p, None, 0, 3, others_sets)
    pass_on(out_p).wait_recv()
    forward_out(take_x, fop, mix_p, put_hidden, do, 0, 3)

    halos = [
        go(hx.at[own, 0], hx.at[own, 4], col_prev),
        go(hx.at[0, own], hx.at[4, own], row_prev),
        go(hx.at[0, 0], hx.at[4, 4], corner_prev),
    ]
    forward_attend(pr_p, es_p, rd_p, mix_p, None, 3, 4, others_sets)
    forward_out(take_x, fop, mix_p, put_hidden, do, 3, 4)

    def take_hidden(w):
        return window(hx, w, 1)

    cot_copy.wait()

    def into_cells(w, carry):
        put_window(cx, w, cells_of(rows_window(cn, w).astype(F32)).astype(BF))
        return carry

    lax.fori_loop(0, 4, into_cells, 0)
    cot_halos = [
        go(cx.at[0, own], cx.at[4, own], row_prev),
        go(cx.at[own, 0], cx.at[own, 4], col_prev),
        go(cx.at[0, 0], cx.at[4, 4], corner_prev),
    ]
    for copy in spread:
        copy.wait()
    spot = fqs.at[:, half_s, away]
    passed_qkv = go(spot, spot, sibling)
    spot = fos.at[half_o]
    passed_out = go(spot, spot, sibling)
    forward_norm(take_hidden, n_s, 0, 1)
    passed_qkv.wait()
    forward_project(n_s, fqs, pr_s, 0, 1)
    cut = (lat * 2 + mp) == 15
    forward_attend(pr_s, es_s, rd_s, mix_s, cut, 0, 1)

    halos[0].wait()
    forward_norm(take_hidden, n_s, 1, 2)
    forward_project(n_s, fqs, pr_s, 1, 2)
    forward_attend(pr_s, es_s, rd_s, mix_s, cut, 1, 2)
    for copy in halos[1:]:
        copy.wait()
    forward_norm(take_hidden, n_s, 2, 4)
    forward_project(n_s, fqs, pr_s, 2, 4)
    forward_attend(pr_s, es_s, rd_s, mix_s, cut, 2, 4)
    passed_out.wait()

    def put_result(w, value):
        put_window(rs, w, value.astype(BF))

    forward_out(take_hidden, fos, mix_s, put_result, do, 0, 4)

    low, high = pl.ds(0, 3), pl.ds(1, 3)

    def narrow(src, dst):
        return [
            go(src.at[3, low], dst.at[0, high], row_next),
            go(src.at[low, 3], dst.at[high, 0], col_next),
            go(src.at[3, 3], dst.at[0, 0], corner_next),
        ]

    result_halos = narrow(rs, rp)
    result_halos.append(keep(rs.at[low, low], rp.at[high, high]))

    def take_cot(w):
        return window(cx, w, 1)

    def put_grad(w, value):
        put_window(gs, w, value.astype(BF))

    def put_shift(kind, j, value):
        g_shift[j, kind // 2, kind % 2] = value.reshape(4, 4, 2, 16, 256)

    for copy in cot_halos:
        copy.wait()
    for first, end in ((1, 4), (0, 1)):
        backward_do(take_cot, fos, cw, do, first, end)
        backward_values(es_s, rd_s, do, ge, dpr, first, end)
        backward_scores(pr_s, es_s, mix_s, ge, dpr, first, end)
        backward_tokens(take_hidden, fqs, cw, dpr, put_grad, do, first, end)
        if first == 1:
            grad_halos = narrow(gs, gp)
    grad_kept = keep(gs.at[low, low], gp.at[high, high])
    backward_out(mix_s, cw, put_shift)
    backward_weights(n_s, dpr, put_shift, (0, 1, 2))
    shifted.step0()
    for copy in result_halos:
        copy.wait()

    def into_rows(w, carry):
        put_rows(rn, w, rows_of(window(rp, w, 0).astype(F32)).astype(BF))
        return carry

    lax.fori_loop(0, 4, into_rows, 0)
    ends = [go(rn.at[:, :, away], ro.at[own_rows], near)]
    ends.append(keep(rn.at[:, :, lanes], ro.at[own_rows]))

    def take_back(w):
        return rows_of(window(gp, w, 0).astype(F32)).astype(BF)

    def put_fields(w, value):
        put_rows(gf, w, value.astype(BF))

    def put_plain(kind, j, value):
        to = g_early if kind >= 2 else g_late
        for part in range(2):
            half = value[:, part * 128 : (part + 1) * 128]
            to[j, kind % 2, part] = half.reshape(4, 4, 2, 16, 128)

    grad_kept.wait()
    backward_do(take_back, fop, cw, do, 3, 4)
    backward_values(es_p, rd_p, do, ge, dpr, 3, 4)
    backward_scores(pr_p, es_p, mix_p, ge, dpr, 3, 4)
    shifted.step1()
    for copy in grad_halos:
        copy.wait()
    backward_do(take_back, fop, cw, do, 0, 3)
    backward_values(es_p, rd_p, do, ge, dpr, 0, 3)
    backward_weights(n_p, dpr, put_plain, (2,))
    backward_out(mix_p, cw, put_plain)
    early.step0()
    backward_scores(pr_p, es_p, mix_p, ge, dpr, 0, 3)
    early.step1()
    backward_weights(n_p, dpr, put_plain, (0, 1))
    late.step0()
    for half in range(2):
        backward_tokens(take_x, fqp, cw, dpr, put_fields, do, half * 2, half * 2 + 2)
        rows = pl.ds(half * 8, 8)
        there = pl.ds(mp * 16 + half * 8, 8)
        ends.append(go(gf.at[rows, :, away], gfo.at[there], near))
        ends.append(keep(gf.at[rows, :, lanes], gfo.at[there]))
        if half == 0:
            late.step1()
            shifted.step2()
    early.step2()
    shifted.step3()
    late.step2()
    early.step3()
    shifted.step4()
    late.step3()
    early.step4()
    shifted.step5()
    late.step4()
    early.step5()
    shifted.step6()
    late.step5()
    early.step6()
    late.step6()
    shifted.last()
    early.last()
    late.last()
    for copy in ends:
        copy.wait()
    for copy in unsent:
        copy.wait_send()


def last_kernel(
    factor, f_early, f_late, f_shift, r, gf,
    qkv_p, out_p, qkv_s, out_s, ro, gfo,
    raw, wide, held, came, gone,
):
    coming, going = [], []

    def move(src, dst, sem, to):
        copy = pltpu.make_async_copy(src, dst, sem)
        copy.start()
        to.append(copy)

    for n in range(4):
        move(f_shift.at[pl.ds(n * 512, 512)], raw.at[n], came.at[n], coming)
    for n, src in enumerate((r, gf)):
        move(src, held.at[n], came.at[4 + n], coming)
    for n in range(4):
        for part in range(2):
            src = (f_late, f_early)[n // 2].at[n % 2, part]
            dst = raw.at[4 + n, :, pl.ds(part * 128, 128)]
            move(src, dst, came.at[6 + n * 2 + part], coming)
    for n in range(8):
        if n < 4:
            coming[n].wait()
        else:
            coming[n * 2 - 2].wait()
            coming[n * 2 - 1].wait()
        wide[n] = raw[n].astype(F32) * factor
        if n % 4 < 3:
            move(wide.at[n], (qkv_s, qkv_p)[n // 4].at[n % 4], gone.at[n], going)
        else:
            for k in range(2):
                cols = pl.ds(k * 256, 256)
                dst = (out_s, out_p)[n // 4].at[:, cols]
                move(wide.at[n, cols], dst, gone.at[8 + n // 4 * 2 + k], going)
    for n, dst in enumerate((ro, gfo)):
        coming[4 + n].wait()
        move(held.at[n], dst, gone.at[12 + n], going)
    for copy in going:
        copy.wait()


def shape(*dims, dtype=BF):
    return jax.ShapeDtypeStruct(dims, dtype)


GRID = (4, 4, 32, 512)
WIDE = (5, 5, 32, 512)
ROWS = (16, 32, 512)
HELD = (32, 32, 256)
SAVED = (
    ((4, 128, 512), BF),
    ((4, 128, 1536), BF),
    ((4, 4, 128, 512), BF),
    ((4, 128, 512), F32),
    ((4, 128, 512), BF),
)


def sum_shapes(width):
    return [
        (2, 2, 4, 4, 2, 16, width),
        (2, 2, 4, 4, 2, 16, width),
        (2, 3, 2, 4, 2, 16, width),
        (2, 2, 4, 2, 16, width),
        (2, 3, 2, 2, 16, width),
        (2, 2, 2, 16, width),
        (3, 2, 2, 16, width),
    ]


SCRATCH = (
    [(s, BF) for s in (ROWS, WIDE, WIDE, GRID, GRID, GRID, GRID, ROWS, ROWS)]
    + [((3, 512, 512), BF), ((512, 512), BF)] * 2
    + list(SAVED) * 2
    + [((4, 128, 512), BF), ((4, 128, 512), F32), ((4, 128, 1536), BF), ((4, 128, 512), BF), (ROWS, BF)]
    + [((2, 2, 2, 4, 4, 2, 16, width), BF) for width in (128, 128, 256)]
    + [(s, BF) for width in (128, 128, 256) for s in sum_shapes(width)]
)


def on_device(fields, qkv_plain, out_plain, qkv_shift, out_shift, cotangent):
    factor = (fields.shape[0] * fields.shape[1] * 64) ** -0.5
    vmem = pl.BlockSpec(memory_space=pltpu.VMEM)
    hbm = pl.BlockSpec(memory_space=pl.ANY)
    f_half, f_whole = (2, 2, 4, 4, 2, 16, 128), (2, 2, 4, 4, 2, 16, 256)
    result, grad_fields, f_early, f_late, f_shift = pl.pallas_call(
        pair_kernel,
        out_shape=[shape(*HELD), shape(*HELD), shape(*f_half), shape(*f_half), shape(*f_whole)],
        in_specs=[hbm] * 6,
        out_specs=[vmem] * 5,
        scratch_shapes=[pltpu.VMEM(s, t) for s, t in SCRATCH]
        + [
            pltpu.SemaphoreType.DMA((SENDS,)),
            pltpu.SemaphoreType.DMA((SENDS,)),
            pltpu.SemaphoreType.DMA((12,)),
        ],
        compiler_params=pltpu.CompilerParams(
            collective_id=0, has_side_effects=True, vmem_limit_bytes=VMEM_LIMIT
        ),
    )(
        fields,
        cotangent,
        qkv_plain.transpose(1, 0, 2),
        out_plain,
        qkv_shift.transpose(1, 0, 2),
        out_shift,
    )
    qkv, out = shape(3, 512, 256, dtype=F32), shape(256, 512, dtype=F32)
    qkv_p, out_p, qkv_s, out_s, result, grad_fields = pl.pallas_call(
        functools.partial(last_kernel, factor),
        out_shape=[qkv, out, qkv, out, shape(*HELD), shape(*HELD)],
        in_specs=[hbm] * 5,
        out_specs=[hbm] * 6,
        scratch_shapes=[
            pltpu.VMEM((8, 512, 256), BF),
            pltpu.VMEM((8, 512, 256), F32),
            pltpu.VMEM((2,) + HELD, BF),
            pltpu.SemaphoreType.DMA((14,)),
            pltpu.SemaphoreType.DMA((14,)),
        ],
        compiler_params=pltpu.CompilerParams(vmem_limit_bytes=VMEM_LIMIT),
    )(
        f_early.reshape(2, 2, 512, 128),
        f_late.reshape(2, 2, 512, 128),
        f_shift.reshape(2048, 256),
        result,
        grad_fields,
    )
    return (
        result,
        grad_fields,
        qkv_p.transpose(1, 0, 2),
        out_p,
        qkv_s.transpose(1, 0, 2),
        out_s,
    )


def solution(mesh):
    in_specs = (
        P("lat", "lon", "mp"),
        P(None, None, "mp"),
        P("mp", None),
        P(None, None, "mp"),
        P("mp", None),
        P("lat", "lon", "mp"),
    )
    out_specs = (
        P("lat", "lon", "mp"),
        P("lat", "lon", "mp"),
        P(None, None, "mp"),
        P("mp", None),
        P(None, None, "mp"),
        P("mp", None),
    )
    return jax.shard_map(
        on_device, mesh=mesh, in_specs=in_specs, out_specs=out_specs, check_vma=False
    )
```

```python
import functools

import jax
import jax.numpy as jnp
from jax import lax
from jax.experimental import pallas as pl
from jax.experimental.pallas import tpu as pltpu
from jax.sharding import PartitionSpec as P

BF = jnp.bfloat16
F32 = jnp.float32
MESH = pl.DeviceIdType.MESH
VMEM_LIMIT = 56 * 1024 * 1024
D = 512
HEAD_DIM = 32
SCALE = HEAD_DIM ** -0.5
LOG2E = 1.4426950408889634


def place():
    lat, lon, mp = lax.axis_index("lat"), lax.axis_index("lon"), lax.axis_index("mp")
    return lat, lon, mp


def row_step(lat, mp, step):
    at = lax.rem(lat * 2 + mp + step + 16, 16)
    return at // 2, lax.rem(at, 2)


def barrier(peers):
    sem = pltpu.get_barrier_semaphore()
    for peer in peers:
        pl.semaphore_signal(sem, inc=1, device_id=peer, device_id_type=MESH)
    pl.semaphore_wait(sem, len(peers))


class Sender:
    def __init__(self, send, recv):
        self.send, self.recv, self.used = send, recv, 0

    def __call__(self, src, dst, peer):
        copy = pltpu.make_async_remote_copy(
            src_ref=src,
            dst_ref=dst,
            send_sem=self.send.at[self.used],
            recv_sem=self.recv.at[self.used],
            device_id=peer,
            device_id_type=MESH,
        )
        self.used += 1
        copy.start()
        return copy


NN = (((1,), (0,)), ((), ()))
NT = (((1,), (1,)), ((), ()))
TN = (((0,), (0,)), ((), ()))


def dot(left, right, dims=NN):
    return lax.dot_general(left, right, dims, preferred_element_type=F32)


def head_masks():
    lane = lax.broadcasted_iota(jnp.int32, (128, 128), 1) // HEAD_DIM
    return [lane == h for h in range(4)]


def spread_heads(block, masks):
    zero = jnp.zeros_like(block)
    return jnp.concatenate([jnp.where(m, block, zero) for m in masks], 0)


def merge_heads(tall, masks):
    total = jnp.where(masks[0], tall[0:128], 0.0)
    for h in range(1, 4):
        total = jnp.where(masks[h], tall[h * 128 : (h + 1) * 128], total)
    return total


def standardize(x):
    centred = x - jnp.mean(x, -1, keepdims=True)
    inv = lax.rsqrt(jnp.mean(centred * centred, -1, keepdims=True) + 1e-05)
    return centred * inv, inv


def window(ref, w, offset):
    i, j = w // 2, lax.rem(w, 2)
    got = ref[pl.ds(2 * i + offset, 2), pl.ds(2 * j + offset, 2)]
    return got.reshape(128, D)


def put_window(ref, w, value):
    i, j = w // 2, lax.rem(w, 2)
    ref[pl.ds(2 * i, 2), pl.ds(2 * j, 2)] = value.reshape(2, 2, 32, D)


def rows_window(ref, w):
    i, j = w // 2, lax.rem(w, 2)
    got = ref[pl.ds(8 * i, 8), pl.ds(pl.multiple_of(16 * j, 16), 16)]
    return got.reshape(128, D)


def put_rows(ref, w, value):
    i, j = w // 2, lax.rem(w, 2)
    ref[pl.ds(8 * i, 8), pl.ds(pl.multiple_of(16 * j, 16), 16)] = value.reshape(8, 16, D)


def cells_of(value):
    return value.reshape(2, 4, 2, 8, D).transpose(0, 2, 1, 3, 4).reshape(128, D)


def rows_of(value):
    return value.reshape(2, 2, 4, 8, D).transpose(0, 2, 1, 3, 4).reshape(128, D)


def forward_norm(take, n, low, high):
    def norm(w, carry):
        n[w] = standardize(take(w).astype(F32))[0].astype(BF)
        return carry

    lax.fori_loop(low, high, norm, 0)


def lanes_at(start, size):
    if isinstance(start, int):
        return slice(start, start + size)
    return pl.ds(pl.multiple_of(start, size), size)


def forward_project(n, wq, pr, low, high, groups=(0, 1)):
    count = high - low
    for j in groups:
        for c in range(3):
            weight = wq[c, :, lanes_at(j * 256, 256)]
            got = dot(n[low:high].reshape(count * 128, 512), weight)
            pr[low:high, :, lanes_at(c * 512 + j * 256, 256)] = got.astype(BF).reshape(count, 128, 256)


def forward_attend(pr, es, rd, mix, cut, low, high, chosen=(0, 1, 2, 3)):
    masks = head_masks()
    ones = spread_heads(jnp.ones((128, 128), BF), masks)
    if cut is not None:
        q_half = lax.broadcasted_iota(jnp.int32, (128, 512), 0) // 64
        k_half = lax.rem(lax.broadcasted_iota(jnp.int32, (128, 512), 1) // 64, 2)
        same = q_half == k_half

    def attend(w, carry):
        scores = []
        for s in chosen:
            q = pr[w, :, lanes_at(s * 128, 128)]
            k = spread_heads(pr[w, :, lanes_at(512 + s * 128, 128)], masks)
            scores.append(dot(q, k, NT))
        es_now = []
        for score in scores:
            e = jnp.exp2(score * (SCALE * LOG2E))
            if cut is not None:
                e = jnp.where(same | jnp.logical_not(cut & (w >= 2)), e, 0.0)
            es_now.append(e.astype(BF))
        both = []
        for s, e in zip(chosen, es_now):
            v = spread_heads(pr[w, :, lanes_at(1024 + s * 128, 128)], masks)
            both.append(dot(e, jnp.concatenate([v, ones], 1)))
        for s, e, pair in zip(chosen, es_now, both):
            es[w, s] = e
            inv = 1.0 / pair[:, 128:]
            rd[w, :, lanes_at(s * 128, 128)] = inv
            mix[w, :, lanes_at(s * 128, 128)] = (pair[:, :128] * inv).astype(BF)
        return carry

    lax.fori_loop(low, high, attend, 0, unroll=2 if (high - low) % 2 == 0 else 1)


def forward_out(take, wo, mix, put, work, low, high):
    count = high - low
    got = dot(mix[low:high].reshape(count * 128, 512), wo[...])
    work[low:high] = got.reshape(count, 128, 512)

    def project(w, carry):
        put(w, take(w).astype(F32) + work[w])
        return carry

    lax.fori_loop(low, high, project, 0)


def backward_do(take, wo, cw, do, low, high):
    count = high - low

    def gather(w, carry):
        cw[w] = take(w)
        return carry

    lax.fori_loop(low, high, gather, 0)
    for j in range(2):
        cols = slice(j * 256, (j + 1) * 256)
        got = dot(cw[low:high].reshape(count * 128, 512), wo[cols, :], NT)
        do[low:high, :, cols] = got.reshape(count, 128, 256)


def backward_out(mix, cw, put):
    for j in range(2):
        cols = slice(j * 256, (j + 1) * 256)
        got = dot(mix[:, :, cols].reshape(512, 256), cw[...].reshape(512, 512), TN).astype(BF)
        put(3, j, jnp.concatenate([got[:, 0:256], got[:, 256:512]], 0))


def backward_values(es, rd, do, ge, dpr, low, high):
    masks = head_masks()

    def attend(w, carry):
        sets = [slice(s * 128, (s + 1) * 128) for s in range(4)]
        g1 = [(do[w, :, lanes] * rd[w, :, lanes]).astype(BF) for lanes in sets]
        tall = [dot(es[w, s], g1[s], TN) for s in range(4)]
        for s in range(4):
            ge[w, :, sets[s]] = g1[s]
            dv = merge_heads(tall[s], masks)
            dpr[w, :, 1024 + s * 128 : 1024 + (s + 1) * 128] = dv.astype(BF)
        return carry

    lax.fori_loop(low, high, attend, 0, unroll=2 if (high - low) % 2 == 0 else 1)


def backward_scores(pr, es, mix, ge, dpr, low, high):
    masks = head_masks()
    ones = spread_heads(jnp.ones((128, 128), BF), masks)

    def attend(w, carry):
        sets = [slice(s * 128, (s + 1) * 128) for s in range(4)]
        t = []
        for s in range(4):
            v = spread_heads(pr[w, :, 1024 + s * 128 : 1024 + (s + 1) * 128], masks)
            g1 = ge[w, :, sets[s]]
            g2 = (-(g1.astype(F32) * mix[w, :, sets[s]].astype(F32))).astype(BF)
            t.append(dot(jnp.concatenate([g1, g2], 1), jnp.concatenate([v, ones], 1), NT))
        ds = [(es[w, s].astype(F32) * t[s]).astype(BF) for s in range(4)]
        dq, dk = [], []
        for s in range(4):
            k = spread_heads(pr[w, :, 512 + s * 128 : 512 + (s + 1) * 128], masks)
            dq.append(dot(ds[s], k) * SCALE)
            dk.append(merge_heads(dot(ds[s], pr[w, :, sets[s]], TN), masks) * SCALE)
        for s in range(4):
            dpr[w, :, sets[s]] = dq[s].astype(BF)
            dpr[w, :, 512 + s * 128 : 512 + (s + 1) * 128] = dk[s].astype(BF)
        return carry

    lax.fori_loop(low, high, attend, 0, unroll=2 if (high - low) % 2 == 0 else 1)


def backward_weights(n, dpr, put, kinds):
    for c in kinds:
        for j in range(2):
            cols = slice(c * 512 + j * 256, c * 512 + (j + 1) * 256)
            got = dot(n[...].reshape(512, 512), dpr[:, :, cols].reshape(512, 256), TN)
            put(c, j, got.astype(BF))


def backward_tokens(take, wq, cw, dpr, put, work, low, high):
    count = high - low
    grad = dot(dpr[low:high, :, 0:512].reshape(count * 128, 512), wq[0], NT)
    for c in (1, 2):
        part = dpr[low:high, :, c * 512 : (c + 1) * 512].reshape(count * 128, 512)
        grad = grad + dot(part, wq[c], NT)
    work[low:high] = grad.reshape(count, 128, 512)

    def finish(w, carry):
        grad = work[w]
        standard, inv = standardize(take(w).astype(F32))
        back = inv * (
            grad
            - jnp.mean(grad, -1, keepdims=True)
            - standard * jnp.mean(grad * standard, -1, keepdims=True)
        )
        put(w, cw[w].astype(F32) + back)
        return carry

    lax.fori_loop(low, high, finish, 0)


class Sum:
    def __init__(self, go, g, f, r0, a0, r1, a1, r2, a2, r3):
        self.go, self.g, self.f = go, g, f
        self.r0, self.a0, self.r1, self.a1, self.r2, self.a2, self.r3 = r0, a0, r1, a1, r2, a2, r3
        lat, lon, mp = place()
        self.mp, self.core, z = mp, lax.rem(lon, 2), lon // 2
        y, self.x_hi = lax.rem(lat, 4), lat // 4
        self.near = (lat, lon, 1 - mp)
        self.far = (lax.rem(lat + 4, 8), lon, 1 - mp)
        self.opposite = (lax.rem(lat + 4, 8), lon, mp)
        self.sibling = (lat, lon + 1 - 2 * self.core, mp)

        def along_y(step):
            return (lat // 4 * 4 + lax.rem(y + step, 4), lon, mp)

        def along_z(step):
            return (lat, lax.rem(z + step, 4) * 2 + lax.rem(lon, 2), mp)

        self.ways = ((y, along_y, z, along_z), (z, along_z, y, along_y))
        self.peers = [self.near, self.far, self.opposite, self.sibling]
        self.peers += [along_y(s) for s in (1, 2, 3)] + [along_z(s) for s in (1, 2, 3)]
        self.flying = []

    def wait(self):
        for copy in self.flying:
            copy.wait()
        self.flying = []

    def step0(self):
        self.flying = [self.go(self.g.at[:, 1 - self.core], self.r0, self.sibling)]

    def step1(self):
        self.wait()
        g, r0, a0, core = self.g, self.r0, self.a0, self.core

        def fold(n, carry):
            part, a = n // 4, lax.rem(n, 4)
            mine = g[:, core, part, a].astype(F32)
            a0[:, part, a] = (mine + r0[:, part, a].astype(F32)).astype(BF)
            return carry

        lax.fori_loop(0, 8, fold, 0)
        for step in (1, 2, 3):
            for part, (ia, along_a, ib, along_b) in enumerate(self.ways):
                to = lax.rem(ia + step, 4)
                self.flying.append(
                    self.go(a0.at[:, part, to], self.r1.at[part, step - 1], along_a(step))
                )

    def step2(self):
        self.wait()
        a0, r1, a1 = self.a0, self.r1, self.a1
        for part, (ia, along_a, ib, along_b) in enumerate(self.ways):

            def fold(b, carry):
                total = a0[:, part, ia, b].astype(F32)
                for k in range(3):
                    total = total + r1[part, k, :, b].astype(F32)
                a1[:, part, b] = total.astype(BF)
                return carry

            lax.fori_loop(0, 4, fold, 0)
        for step in (1, 2, 3):
            for part, (ia, along_a, ib, along_b) in enumerate(self.ways):
                to = lax.rem(ib + step, 4)
                self.flying.append(
                    self.go(a1.at[:, part, to], self.r2.at[part, step - 1], along_b(step))
                )

    def step3(self):
        self.wait()
        a1, r2, a2, r3, mp = self.a1, self.r2, self.a2, self.r3, self.mp
        for part, (ia, along_a, ib, along_b) in enumerate(self.ways):
            total = a1[:, part, ib].astype(F32)
            for k in range(3):
                total = total + r2[part, k].astype(F32)
            a2[:, part] = total.astype(BF)
        self.flying = [
            self.go(a2.at[1 - mp], r3.at[0], self.near),
            self.go(a2.at[1 - mp], r3.at[1], self.far),
            self.go(a2.at[mp], r3.at[2], self.opposite),
        ]

    def step4(self):
        self.wait()
        same = self.a2[self.mp].astype(F32) + self.r3[2].astype(F32)
        other = self.r3[0].astype(F32) + self.r3[1].astype(F32)
        total = (same + other).astype(BF)
        for part, (ia, along_a, ib, along_b) in enumerate(self.ways):
            self.f[self.core, part, ia, ib] = total[part]
        for step in (1, 2, 3):
            for part, (ia, along_a, ib, along_b) in enumerate(self.ways):
                spot = self.f.at[self.core, part, ia, ib]
                self.flying.append(self.go(spot, spot, along_b(step)))

    def step5(self):
        self.wait()
        self.coming = []
        for step in (1, 2, 3):
            for part, (ia, along_a, ib, along_b) in enumerate(self.ways):
                spot = self.f.at[self.core, part, ia]
                arrives = self.f.at[self.core, part, lax.rem(ia + 4 - step, 4)]
                self.coming.append((self.go(spot, spot, along_a(step)), arrives))
        for part, (ia, along_a, ib, along_b) in enumerate(self.ways):
            spot = self.f.at[self.core, part, ia]
            self.flying.append(self.go(spot, spot, self.sibling))

    def step6(self):
        for copy, spot in self.coming:
            copy.wait_recv()
            self.flying.append(self.go(spot, spot, self.sibling))

    def last(self):
        self.wait()
        for copy, _ in self.coming:
            copy.wait_send()


def around(lat, lon, mp, step):
    row_lat, row_mp = row_step(lat, mp, step)
    col = lax.rem(lon + step + 8, 8)
    return (row_lat, lon, row_mp), (lat, col, mp), (row_lat, col, row_mp)


SENDS = 176


def pair_kernel(
    fc, cc, wqp, wop, wqs, wos,
    ro, gfo, f_early_out, f_late_out, f_shift_out,
    f_early, f_late, f_shift, x, hx, cx, rs, rp, gs, gp, gf, rn,
    fqp, fop, fqs, fos,
    n_p, pr_p, es_p, rd_p, mix_p,
    n_s, pr_s, es_s, rd_s, mix_s,
    cw, do, dpr, ge, cn,
    g_early, g_late, g_shift,
    *rest,
):
    sums, (send, recv, local) = rest[:21], rest[21:]
    lat, lon, mp = place()
    row_prev, col_prev, corner_prev = around(lat, lon, mp, -1)
    row_next, col_next, corner_next = around(lat, lon, mp, 1)
    go = Sender(send, recv)
    early = Sum(go, g_early, f_early, *sums[:7])
    late = Sum(go, g_late, f_late, *sums[7:14])
    shifted = Sum(go, g_shift, f_shift, *sums[14:])
    near, far, sibling, core = early.near, early.far, early.sibling, early.core
    barrier(
        early.peers
        + [row_prev, col_prev, corner_prev, row_next, col_next, corner_next]
    )
    lanes = pl.ds(pl.multiple_of(mp * 256, 256), 256)
    away = pl.ds(pl.multiple_of((1 - mp) * 256, 256), 256)
    other_rows = pl.ds((1 - mp) * 16, 16)
    other_half = [pl.ds((1 - mp) * 16 + half * 8, 8) for half in range(2)]
    own_rows = pl.ds(mp * 16, 16)
    own = pl.ds(0, 4)
    kept = []

    def keep(src, dst):
        copy = pltpu.make_async_copy(src, dst, local.at[len(kept)])
        copy.start()
        kept.append(copy)
        return copy

    def weight(src, dst, c, peer):
        rows = pl.ds(pl.multiple_of(core * 256, 256), 256)
        return go(src.at[c, rows], dst.at[c, rows, lanes], peer), dst.at[c, rows, away]

    def weight_out(src, dst, peer):
        rows = pl.ds(pl.multiple_of(core * 128, 128), 128)
        there = pl.ds(pl.multiple_of(mp * 256 + core * 128, 128), 128)
        here = pl.ds(pl.multiple_of((1 - mp) * 256 + core * 128, 128), 128)
        return go(src.at[rows], dst.at[there], peer), dst.at[here]

    y, z = lax.rem(lat, 4), lon // 2
    along_y, along_z = early.ways[0][1], early.ways[0][3]
    rows_s = pl.ds(pl.multiple_of(core * 256 + y * 64, 64), 64)
    half_s = pl.ds(pl.multiple_of(core * 256, 256), 256)
    at_o = core * 128 + z * 32
    rows_o = pl.ds(pl.multiple_of(at_o, 32), 32)
    there_o = pl.ds(pl.multiple_of(mp * 256 + at_o, 32), 32)
    here_o = pl.ds(pl.multiple_of((1 - mp) * 256 + at_o, 32), 32)
    half_o = pl.ds(pl.multiple_of((1 - mp) * 256 + core * 128, 128), 128)

    unsent = []

    def pass_on(part):
        copy, spot = part
        copy.wait_recv()
        unsent.append(copy)
        passed = go(spot, spot, sibling)
        unsent.append(passed)
        return passed

    fields_copy = [
        go(fc.at[other_half[half]], x.at[pl.ds(half * 8, 8), :, lanes], near) for half in range(2)
    ]
    qkv_p = [weight(wqp, fqp, c, far) for c in range(3)]
    out_p = weight_out(wop, fop, far)
    over_x = [
        go(wqs.at[:, rows_s], fqs.at[:, rows_s, lanes], near),
        go(wos.at[rows_o], fos.at[there_o], near),
    ]
    cot_copy = go(cc.at[other_rows], cn.at[:, :, lanes], near)
    x_kept = keep(fc.at[own_rows], x.at[:, :, lanes])
    mp_rows = pl.ds(pl.multiple_of(mp * 256, 256), 256)
    others = [
        keep(wqp, fqp.at[:, :, lanes]),
        keep(wop, fop.at[mp_rows]),
        keep(wqs, fqs.at[:, :, lanes]),
        keep(wos, fos.at[mp_rows]),
        keep(cc.at[own_rows], cn.at[:, :, lanes]),
    ]

    def take_x(w):
        return rows_window(x, w)

    def put_hidden(w, value):
        put_window(hx, w, cells_of(value).astype(BF))

    x_kept.wait()
    for half in range(2):
        fields_copy[half].wait()
        forward_norm(take_x, n_p, half * 2, half * 2 + 2)
        if half == 0:
            for copy in others:
                copy.wait()
        forward_project(n_p, fqp, pr_p, half * 2, half * 2 + 2, (mp,))
    passed = [pass_on(part) for part in qkv_p]
    for copy in over_x:
        copy.wait_recv()
    unsent.extend(over_x)
    spread = []
    for step in (1, 2, 3):
        spot = fqs.at[:, rows_s, away]
        spread.append(go(spot, spot, along_y(step)))
        spot = fos.at[here_o]
        spread.append(go(spot, spot, along_z(step)))
    forward_attend(pr_p, es_p, rd_p, mix_p, None, 0, 4, (mp * 2, mp * 2 + 1))
    for copy in passed:
        copy.wait_recv()
    forward_project(n_p, fqp, pr_p, 0, 4, (1 - mp,))
    others_sets = (2 - mp * 2, 3 - mp * 2)
    forward_attend(pr_p, es_p, rd_p, mix_p, None, 0, 3, others_sets)
    pass_on(out_p).wait_recv()
    forward_out(take_x, fop, mix_p, put_hidden, do, 0, 3)

    halos = [
        go(hx.at[own, 0], hx.at[own, 4], col_prev),
        go(hx.at[0, own], hx.at[4, own], row_prev),
        go(hx.at[0, 0], hx.at[4, 4], corner_prev),
    ]
    forward_attend(pr_p, es_p, rd_p, mix_p, None, 3, 4, others_sets)
    forward_out(take_x, fop, mix_p, put_hidden, do, 3, 4)

    def take_hidden(w):
        return window(hx, w, 1)

    cot_copy.wait()

    def into_cells(w, carry):
        put_window(cx, w, cells_of(rows_window(cn, w).astype(F32)).astype(BF))
        return carry

    lax.fori_loop(0, 4, into_cells, 0)
    cot_halos = [
        go(cx.at[0, own], cx.at[4, own], row_prev),
        go(cx.at[own, 0], cx.at[own, 4], col_prev),
        go(cx.at[0, 0], cx.at[4, 4], corner_prev),
    ]
    for copy in spread:
        copy.wait()
    spot = fqs.at[:, half_s, away]
    passed_qkv = go(spot, spot, sibling)
    spot = fos.at[half_o]
    passed_out = go(spot, spot, sibling)
    forward_norm(take_hidden, n_s, 0, 1)
    passed_qkv.wait()
    forward_project(n_s, fqs, pr_s, 0, 1)
    cut = (lat * 2 + mp) == 15
    forward_attend(pr_s, es_s, rd_s, mix_s, cut, 0, 1)

    halos[0].wait()
    forward_norm(take_hidden, n_s, 1, 2)
    forward_project(n_s, fqs, pr_s, 1, 2)
    forward_attend(pr_s, es_s, rd_s, mix_s, cut, 1, 2)
    for copy in halos[1:]:
        copy.wait()
    forward_norm(take_hidden, n_s, 2, 4)
    forward_project(n_s, fqs, pr_s, 2, 4)
    forward_attend(pr_s, es_s, rd_s, mix_s, cut, 2, 4)
    passed_out.wait()

    def put_result(w, value):
        put_window(rs, w, value.astype(BF))

    forward_out(take_hidden, fos, mix_s, put_result, do, 0, 4)

    low, high = pl.ds(0, 3), pl.ds(1, 3)

    def narrow(src, dst):
        return [
            go(src.at[3, low], dst.at[0, high], row_next),
            go(src.at[low, 3], dst.at[high, 0], col_next),
            go(src.at[3, 3], dst.at[0, 0], corner_next),
        ]

    result_halos = narrow(rs, rp)
    result_halos.append(keep(rs.at[low, low], rp.at[high, high]))

    def take_cot(w):
        return window(cx, w, 1)

    def put_grad(w, value):
        put_window(gs, w, value.astype(BF))

    def put_shift(kind, j, value):
        g_shift[j, kind // 2, kind % 2] = value.reshape(4, 4, 2, 16, 256)

    for copy in cot_halos:
        copy.wait()
    for first, end in ((1, 4), (0, 1)):
        backward_do(take_cot, fos, cw, do, first, end)
        backward_values(es_s, rd_s, do, ge, dpr, first, end)
        backward_scores(pr_s, es_s, mix_s, ge, dpr, first, end)
        backward_tokens(take_hidden, fqs, cw, dpr, put_grad, do, first, end)
        if first == 1:
            grad_halos = narrow(gs, gp)
    grad_kept = keep(gs.at[low, low], gp.at[high, high])
    backward_out(mix_s, cw, put_shift)
    backward_weights(n_s, dpr, put_shift, (0, 1, 2))
    shifted.step0()
    for copy in result_halos:
        copy.wait()

    def into_rows(w, carry):
        put_rows(rn, w, rows_of(window(rp, w, 0).astype(F32)).astype(BF))
        return carry

    lax.fori_loop(0, 4, into_rows, 0)
    ends = [go(rn.at[:, :, away], ro.at[own_rows], near)]
    ends.append(keep(rn.at[:, :, lanes], ro.at[own_rows]))

    def take_back(w):
        return rows_of(window(gp, w, 0).astype(F32)).astype(BF)

    def put_fields(w, value):
        put_rows(gf, w, value.astype(BF))

    def put_plain(kind, j, value):
        to = g_early if kind >= 2 else g_late
        for part in range(2):
            half = value[:, part * 128 : (part + 1) * 128]
            to[j, kind % 2, part] = half.reshape(4, 4, 2, 16, 128)

    grad_kept.wait()
    backward_do(take_back, fop, cw, do, 3, 4)
    backward_values(es_p, rd_p, do, ge, dpr, 3, 4)
    backward_scores(pr_p, es_p, mix_p, ge, dpr, 3, 4)
    shifted.step1()
    for copy in grad_halos:
        copy.wait()
    backward_do(take_back, fop, cw, do, 0, 3)
    backward_values(es_p, rd_p, do, ge, dpr, 0, 3)
    backward_weights(n_p, dpr, put_plain, (2,))
    backward_out(mix_p, cw, put_plain)
    early.step0()
    backward_scores(pr_p, es_p, mix_p, ge, dpr, 0, 3)
    early.step1()
    backward_weights(n_p, dpr, put_plain, (0, 1))
    late.step0()
    for half in range(2):
        backward_tokens(take_x, fqp, cw, dpr, put_fields, do, half * 2, half * 2 + 2)
        rows = pl.ds(half * 8, 8)
        there = pl.ds(mp * 16 + half * 8, 8)
        ends.append(go(gf.at[rows, :, away], gfo.at[there], near))
        ends.append(keep(gf.at[rows, :, lanes], gfo.at[there]))
        if half == 0:
            late.step1()
            shifted.step2()
    early.step2()
    shifted.step3()
    late.step2()
    early.step3()
    shifted.step4()
    late.step3()
    early.step4()
    shifted.step5()
    late.step4()
    early.step5()
    shifted.step6()
    late.step5()
    shifted.last()
    ends.append(keep(f_shift, f_shift_out))
    early.step6()
    late.step6()
    early.last()
    ends.append(keep(f_early, f_early_out))
    late.last()
    ends.append(keep(f_late, f_late_out))
    for copy in ends:
        copy.wait()
    for copy in unsent:
        copy.wait_send()


def last_kernel(
    factor, f_early, f_late, f_shift, r, gf,
    qkv_p, out_p, qkv_s, out_s, ro, gfo,
    raw, wide, held, came, gone,
):
    coming, going = [], []

    def move(src, dst, sem, to):
        copy = pltpu.make_async_copy(src, dst, sem)
        copy.start()
        to.append(copy)

    for n in range(4):
        move(f_shift.at[pl.ds(n * 512, 512)], raw.at[n], came.at[n], coming)
    for n, src in enumerate((r, gf)):
        move(src, held.at[n], came.at[4 + n], coming)
    for n in range(4):
        for part in range(2):
            src = (f_late, f_early)[n // 2].at[n % 2, part]
            dst = raw.at[4 + n, :, pl.ds(part * 128, 128)]
            move(src, dst, came.at[6 + n * 2 + part], coming)
    for n in range(8):
        if n < 4:
            coming[n].wait()
        else:
            coming[n * 2 - 2].wait()
            coming[n * 2 - 1].wait()
        wide[n] = raw[n].astype(F32) * factor
        if n % 4 < 3:
            move(wide.at[n], (qkv_s, qkv_p)[n // 4].at[n % 4], gone.at[n], going)
        else:
            for k in range(2):
                cols = pl.ds(k * 256, 256)
                dst = (out_s, out_p)[n // 4].at[:, cols]
                move(wide.at[n, cols], dst, gone.at[8 + n // 4 * 2 + k], going)
    for n, dst in enumerate((ro, gfo)):
        coming[4 + n].wait()
        move(held.at[n], dst, gone.at[12 + n], going)
    for copy in going:
        copy.wait()


def shape(*dims, dtype=BF):
    return jax.ShapeDtypeStruct(dims, dtype)


GRID = (4, 4, 32, 512)
WIDE = (5, 5, 32, 512)
ROWS = (16, 32, 512)
HELD = (32, 32, 256)
SAVED = (
    ((4, 128, 512), BF),
    ((4, 128, 1536), BF),
    ((4, 4, 128, 512), BF),
    ((4, 128, 512), F32),
    ((4, 128, 512), BF),
)


def sum_shapes(width):
    return [
        (2, 2, 4, 4, 2, 16, width),
        (2, 2, 4, 4, 2, 16, width),
        (2, 3, 2, 4, 2, 16, width),
        (2, 2, 4, 2, 16, width),
        (2, 3, 2, 2, 16, width),
        (2, 2, 2, 16, width),
        (3, 2, 2, 16, width),
    ]


SCRATCH = (
    [(s, BF) for s in (ROWS, WIDE, WIDE, GRID, GRID, GRID, GRID, ROWS, ROWS)]
    + [((3, 512, 512), BF), ((512, 512), BF)] * 2
    + list(SAVED) * 2
    + [((4, 128, 512), BF), ((4, 128, 512), F32), ((4, 128, 1536), BF), ((4, 128, 512), BF), (ROWS, BF)]
    + [((2, 2, 2, 4, 4, 2, 16, width), BF) for width in (128, 128, 256)]
    + [(s, BF) for width in (128, 128, 256) for s in sum_shapes(width)]
)


def on_device(fields, qkv_plain, out_plain, qkv_shift, out_shift, cotangent):
    factor = (fields.shape[0] * fields.shape[1] * 64) ** -0.5
    hbm = pl.BlockSpec(memory_space=pl.ANY)
    f_half, f_whole = (2, 2, 4, 4, 2, 16, 128), (2, 2, 4, 4, 2, 16, 256)
    result, grad_fields, f_early, f_late, f_shift = pl.pallas_call(
        pair_kernel,
        out_shape=[shape(*HELD), shape(*HELD), shape(*f_half), shape(*f_half), shape(*f_whole)],
        in_specs=[hbm] * 6,
        out_specs=[hbm] * 5,
        scratch_shapes=[pltpu.VMEM(s, BF) for s in (f_half, f_half, f_whole)]
        + [pltpu.VMEM(s, t) for s, t in SCRATCH]
        + [
            pltpu.SemaphoreType.DMA((SENDS,)),
            pltpu.SemaphoreType.DMA((SENDS,)),
            pltpu.SemaphoreType.DMA((15,)),
        ],
        compiler_params=pltpu.CompilerParams(
            collective_id=0, has_side_effects=True, vmem_limit_bytes=VMEM_LIMIT
        ),
    )(
        fields,
        cotangent,
        qkv_plain.transpose(1, 0, 2),
        out_plain,
        qkv_shift.transpose(1, 0, 2),
        out_shift,
    )
    qkv, out = shape(3, 512, 256, dtype=F32), shape(256, 512, dtype=F32)
    qkv_p, out_p, qkv_s, out_s, result, grad_fields = pl.pallas_call(
        functools.partial(last_kernel, factor),
        out_shape=[qkv, out, qkv, out, shape(*HELD), shape(*HELD)],
        in_specs=[hbm] * 5,
        out_specs=[hbm] * 6,
        scratch_shapes=[
            pltpu.VMEM((8, 512, 256), BF),
            pltpu.VMEM((8, 512, 256), F32),
            pltpu.VMEM((2,) + HELD, BF),
            pltpu.SemaphoreType.DMA((14,)),
            pltpu.SemaphoreType.DMA((14,)),
        ],
        compiler_params=pltpu.CompilerParams(vmem_limit_bytes=VMEM_LIMIT),
    )(
        f_early.reshape(2, 2, 512, 128),
        f_late.reshape(2, 2, 512, 128),
        f_shift.reshape(2048, 256),
        result,
        grad_fields,
    )
    return (
        result,
        grad_fields,
        qkv_p.transpose(1, 0, 2),
        out_p,
        qkv_s.transpose(1, 0, 2),
        out_s,
    )


def solution(mesh):
    in_specs = (
        P("lat", "lon", "mp"),
        P(None, None, "mp"),
        P("mp", None),
        P(None, None, "mp"),
        P("mp", None),
        P("lat", "lon", "mp"),
    )
    out_specs = (
        P("lat", "lon", "mp"),
        P("lat", "lon", "mp"),
        P(None, None, "mp"),
        P("mp", None),
        P(None, None, "mp"),
        P("mp", None),
    )
    return jax.shard_map(
        on_device, mesh=mesh, in_specs=in_specs, out_specs=out_specs, check_vma=False
    )
```
